256 devices in a mesh: dp: 32 (over z, x_lo, core), seq: 8 (over y, x_hi).
Axes of the slice: x: 4 (x_hi: 2, x_lo: 2; x = x_hi * 2 + x_lo), y: 4, z: 8, core: 2. Of those that a mesh axis runs over, the one named last changes fastest.
Arguments:
- hidden: bfloat16 [32, 1024, 8192], P('dp', 'seq'), may hold values from -48 to 48
- w_query: bfloat16 [8192, 128], P('dp'), may hold values from -0.0625 to 0.0625
- w_key: bfloat16 [8192, 128], P('dp'), may hold values from -0.0625 to 0.0625
- w_value: bfloat16 [8192, 128], P('dp'), may hold values from -0.0625 to 0.0625
- score_vec: float32 [128], replicated, may hold values from -4 to 4
- labels: int32 [32], replicated, may hold values from 0 to 1
- lengths: int32 [32], replicated, may hold values from 1 to 8, as said below
- partner: int32 [32], replicated, may hold values from 0 to 31, as said below
Outputs:
- loss: float32 [], replicated
- grad_query: float32 [8192, 128], P('dp')
- grad_key: float32 [8192, 128], P('dp')
- grad_value: float32 [8192, 128], P('dp')
- grad_score: float32 [128], replicated
- grad_hidden: bfloat16 [32, 1024, 8192], P('dp', 'seq')
The draws below stay inside these ranges and needn't reach their ends.
Inputs may be any that keep to these rules, and one draw needn't show every extreme that they name: partner[partner[g]] = g and partner[g] != g; at least one pair joins two neighbouring responses (indices differing by one, counted round). Response g holds 128 * lengths[g] live tokens from its start; some response fills all 8 blocks.
All inputs are finite; a program needn't handle non-finite values.
Results may differ from the reference program's by a relative error of at most 0.033.
Values may be sent and summed in bfloat16 or wider, within the bound.
No kernel may reach another device: no remote copies, remote signals or barrier semaphores. Data moves between devices by JAX's collectives and lax.ppermute only.
A program may use at most 128 MiB of HBM per device.

```python
import math
import jax
import jax.numpy as jnp
from jax import lax

D = 8192
HEAD = 128
BLK = 128
SEQLEN = 1024
NBLK = 8
GROUPS = 32


def draw_hidden(key, part):
    key = jax.random.fold_in(key, 11)
    normal_key = jax.random.fold_in(key, 0)
    base = jax.random.normal(normal_key, (GROUPS, SEQLEN, D), jnp.float32)
    values = base
    return jnp.clip(values, -48.0, 48.0).astype(jnp.bfloat16)


def draw_lengths(key, part):
    key = jax.random.fold_in(key, 23)
    draw_key, pick_key = jax.random.split(key)
    blocks = jax.random.randint(draw_key, (GROUPS,), 1, NBLK + 1, jnp.int32)
    chosen = jax.random.randint(pick_key, (), 0, GROUPS, jnp.int32)
    return jnp.where(jnp.arange(GROUPS) == chosen, NBLK, blocks).astype(jnp.int32)


def draw_partner(key, part):
    key = jax.random.fold_in(key, 37)
    pick_key, order_key = jax.random.split(key)
    first = jax.random.randint(pick_key, (), 0, GROUPS, jnp.int32)
    second = (first + 1) % GROUPS
    others = jax.random.permutation(order_key, GROUPS - 2).astype(jnp.int32)
    rest = (first + 2 + others) % GROUPS
    order = jnp.concatenate([jnp.stack([first, second]), rest]).astype(jnp.int32)
    swapped = order.reshape(GROUPS // 2, 2)[:, ::-1].reshape(GROUPS)
    return jnp.zeros((GROUPS,), jnp.int32).at[order].set(swapped)


def set_ends(values, stream_key, low, top_value):
    longest = values.shape.index(max(values.shape))
    spots = []
    for shift in (0, 1):
        where = [jax.random.randint(jax.random.fold_in(stream_key, axis), (), 0, length) for axis, length in enumerate(values.shape)]
        where[longest] = (where[longest] + shift) % values.shape[longest]
        spots.append(tuple(where))
    return values.at[spots[0]].set(low).at[spots[1]].set(top_value)


def levels(key, extent, pieces, low, largest):
    def one(dim, shards_of):
        draws = jax.random.uniform(jax.random.fold_in(jax.random.fold_in(key, 6), dim), (shards_of,), jnp.float32, low / len(pieces), largest / len(pieces))
        return jnp.repeat(jnp.exp(draws), extent[dim] // shards_of).reshape((-1,) + (1,) * (len(extent) - dim - 1))

    factor_of = one(*pieces[0])
    for cut in pieces[1:]:
        factor_of = factor_of * one(*cut)
    return factor_of


def bell_draw(key, extent, spread, limit, shards=(), dtype=jnp.bfloat16):
    values = jax.random.normal(key, extent, jnp.float32) * spread
    if len(shards) > 0:
        values = levels(key, extent, shards, -0.22, 0.18) * values
    return jnp.clip(values, min=-limit, max=limit).astype(dtype)


def setup_inputs(seed: int = 0) -> dict:
    seeds = jax.random.split(jax.random.key(seed), 9)
    return {
        "hidden": draw_hidden(jax.random.fold_in(seeds[8], 71), 0),
        "w_query": bell_draw(seeds[1], (D, HEAD), D ** -0.5, 0.0625, ((0, 32),)),
        "w_key": bell_draw(seeds[2], (D, HEAD), D ** -0.5, 0.0625, ((0, 32),)),
        "w_value": bell_draw(seeds[3], (D, HEAD), D ** -0.5, 0.0625, ((0, 32),)),
        "score_vec": bell_draw(seeds[4], (HEAD,), 1.0, 4.0, (), jnp.float32),
        "labels": set_ends(jax.random.randint(seeds[5], (GROUPS,), 0, 2), jax.random.fold_in(seeds[5], 1), 0, 1).astype(jnp.int32),
        "lengths": draw_lengths(jax.random.fold_in(seeds[8], 71), 0),
        "partner": draw_partner(jax.random.fold_in(seeds[8], 71), 0),
    }


def group_pass(query, mate_kv, own_len, other_len, label, factor, score_vec):
    length = query.shape[0]
    head = query.shape[1]
    position = jnp.arange(length)
    live = (position < BLK * own_len).astype(jnp.float32)
    usable = position < BLK * other_len
    keys = mate_kv[:, :head]
    values = mate_kv[:, head:]
    scores = jnp.dot(query, keys.T, preferred_element_type=jnp.float32) / math.sqrt(head)
    scores = jnp.where(usable[None, :], scores, jnp.float32(-1e+30))
    top = lax.optimization_barrier(jnp.max(scores, axis=-1, keepdims=True))
    expo = jnp.exp(scores - top)
    probs = expo / lax.optimization_barrier(jnp.sum(expo, axis=-1, keepdims=True))
    probs_b = probs.astype(jnp.bfloat16)
    attended = jnp.dot(probs_b, values, preferred_element_type=jnp.float32)
    token_score = lax.optimization_barrier(jnp.sum(attended * score_vec[None, :], axis=-1))
    count = (BLK * own_len).astype(jnp.float32)
    total = jnp.sum(token_score * live) / jnp.sqrt(count)
    sign = (2 * label - 1).astype(jnp.float32)
    loss_term = factor * jax.nn.softplus(-sign * total)
    grad_total = -factor * sign * jax.nn.sigmoid(-sign * total)
    grad_token = live * grad_total / jnp.sqrt(count)
    grad_readout = lax.optimization_barrier(jnp.sum(attended * grad_token[:, None], axis=0))
    grad_att = (grad_token[:, None] * score_vec[None, :]).astype(jnp.bfloat16)
    grad_vals = jnp.dot(probs_b.T, grad_att, preferred_element_type=jnp.float32)
    grad_prob = jnp.dot(grad_att, values.T, preferred_element_type=jnp.float32)
    grad_scores = probs * (grad_prob - lax.optimization_barrier(jnp.sum(grad_prob * probs, axis=-1, keepdims=True))) / math.sqrt(head)
    grad_scores_b = grad_scores.astype(jnp.bfloat16)
    grad_q = jnp.dot(grad_scores_b, keys, preferred_element_type=jnp.float32).astype(jnp.bfloat16)
    grad_keys = jnp.dot(grad_scores_b.T, query, preferred_element_type=jnp.float32)
    return (loss_term, grad_readout, grad_q, jnp.concatenate([grad_keys, grad_vals], axis=1))

def reference(hidden, w_query, w_key, w_value, score_vec, labels, lengths, partner):
    groups, length, width = hidden.shape
    head = w_query.shape[1]
    stacked = jnp.concatenate([w_query, w_key, w_value], axis=1)
    flat = hidden.reshape(groups * length, width)
    proj = jnp.dot(flat, stacked, preferred_element_type=jnp.float32).astype(jnp.bfloat16)
    proj = proj.reshape(groups, length, 3 * head)
    query = proj[:, :, :head]
    own_kv = proj[:, :, head:]
    mate_kv = jnp.take(own_kv, partner.astype(jnp.int32), axis=0)
    other_len = jnp.take(lengths, partner.astype(jnp.int32), axis=0)
    factors = 32.0 * (1.0 + 2.0 * jnp.arange(groups).astype(jnp.float32) / (groups - 1))

    def one(items):
        return group_pass(items[0], items[1], items[2], items[3], items[4], items[5], score_vec)
    loss_terms, readouts, grad_q, grad_mate = lax.map(one, (query, mate_kv, lengths, other_len, labels, factors))
    kv_grad = jnp.take(grad_mate, partner.astype(jnp.int32), axis=0).astype(jnp.bfloat16)
    grad_all = jnp.concatenate([grad_q, kv_grad], axis=2).reshape(groups * length, 3 * head)
    grad_hidden = jnp.dot(grad_all, stacked.T, preferred_element_type=jnp.float32).astype(jnp.bfloat16)
    grad_weights = jnp.dot(flat.T, grad_all, preferred_element_type=jnp.float32)
    return (jnp.sum(loss_terms), grad_weights[:, :head], grad_weights[:, head:2 * head], grad_weights[:, 2 * head:], lax.optimization_barrier(jnp.sum(readouts, axis=0)), grad_hidden.reshape(groups, length, width))
```

```python
import functools
import math

import jax
import jax.numpy as jnp
from jax import lax
from jax.experimental import pallas as pl
from jax.experimental.pallas import tpu as pltpu
from jax.sharding import Mesh
from jax.sharding import PartitionSpec as P

F32 = jnp.float32
BF16 = jnp.bfloat16
NZ, NX, NC = 8, 2, 2
NDP = NZ * NX * NC
NSEQ = 8
BLK = 128
HEAD = 128
ROWS = 256
EXT = 16
SHARE = ROWS // NSEQ
COLS = NDP * SHARE
SEQLEN = NSEQ * BLK
TB = 256
DP = ("z", "xl", "c")
SEQ = ("y", "xh")
LAST = (((1,), (1,)), ((), ()))
VM = pl.BlockSpec(memory_space=pltpu.VMEM)
SM = pl.BlockSpec(memory_space=pltpu.SMEM)


def call(kernel, outs, ins, scratch=(), flops=0, bytes_accessed=0, name=None):
    return pl.pallas_call(
        kernel,
        out_shape=outs,
        in_specs=[SM if a.dtype == jnp.int32 else VM for a in ins],
        out_specs=jax.tree.map(lambda _: VM, outs),
        scratch_shapes=list(scratch),
        compiler_params=pltpu.CompilerParams(vmem_limit_bytes=50 * 1024 * 1024),
        cost_estimate=pl.CostEstimate(flops=flops, bytes_accessed=bytes_accessed, transcendentals=0),
        name=name,
    )(*ins)


def shape(dims, dtype):
    return jax.ShapeDtypeStruct(dims, dtype)


def halves(x):
    high = x.astype(BF16).astype(F32)
    return high, x - high


def pack_weights(wq, wk, wv, score, out):
    out[0:ROWS, 0:HEAD] = wq[...]
    out[0:ROWS, HEAD : 2 * HEAD] = wk[...]
    s1, rest = halves(score[...])
    s2, s3 = halves(rest)
    row = lax.broadcasted_iota(jnp.int32, (EXT, HEAD), 0)
    lhs = jnp.where(row == 0, s1, jnp.where(row == 1, s2, jnp.where(row == 2, s3, 0.0)))
    product = lax.dot_general(lhs.astype(BF16), wv[...], LAST, preferred_element_type=F32)
    total = jnp.sum(product, axis=0, keepdims=True)
    high, low = halves(total)
    row = lax.broadcasted_iota(jnp.int32, (EXT, ROWS), 0)
    ext = jnp.where((row == 0) | (row == 2), high, jnp.where(row == 1, low, 0.0))
    out[ROWS : ROWS + EXT, :] = ext.astype(BF16)


def split_columns(hidden, out):
    size = 4 * BLK
    o = lax.broadcasted_iota(jnp.int32, (size, size), 0)
    i = lax.broadcasted_iota(jnp.int32, (size, size), 1)
    source = BLK * ((o & 127) >> 5) + SHARE * (o >> 7) + (o & 31)
    perm = jnp.where(i == source, 1.0, 0.0).astype(BF16)
    for q in range(NDP // 4):
        for h in range(2):
            parts = [hidden[:, ROWS * (4 * q + k) + BLK * h :][:, :BLK] for k in range(4)]
            x = jnp.concatenate(parts, axis=1)
            y = lax.dot_general(perm, x, LAST, preferred_element_type=F32).astype(BF16)
            for r in range(4):
                out[4 * h + r, BLK * q : BLK * (q + 1), :] = y[BLK * r : BLK * (r + 1)]


def project(ids, hidden, *refs):
    blocks, out = refs[:-1], refs[-1]
    acc = jnp.zeros((BLK, 2 * HEAD), F32)
    wide = jnp.zeros((EXT, BLK), F32)
    for n, block in enumerate(blocks):
        start = pl.multiple_of(ids[n] * ROWS, ROWS)
        x = hidden[:, pl.ds(start, ROWS)]
        acc += jnp.dot(x, block[0:ROWS, :], preferred_element_type=F32)
        wide += lax.dot_general(block[ROWS : ROWS + EXT, :], x, LAST, preferred_element_type=F32)
    qk = acc.astype(BF16)
    high, low = halves(wide[0:1] + wide[1:2])
    row = lax.broadcasted_iota(jnp.int32, (EXT, 2 * HEAD), 0)
    ext = jnp.where(row == 0, jnp.concatenate([high, low], axis=1), 0.0).astype(BF16)
    for s in range(NSEQ):
        out[s, 0:BLK, :] = qk
        out[s, BLK : BLK + EXT, :] = ext


def pick_for_planes(ids, a, b, c, d, out, items):
    for n, ref in enumerate((a, b, c, d)):
        items[n] = ref[...]
    for z in range(NZ):
        out[z] = items[ids[z]]


def pick_partner(ids, received, out):
    mine = received[ids[0]]
    for s in range(NSEQ):
        out[s] = mine


def attention(ids, own, mate, grads, crows, loss, q_t, k_t, q_own, k_own, q_mate, k_mate, wcol, scores, dots, dq, dk, cacc):
    scale = 1.0 / math.sqrt(HEAD)
    exponent = scale * math.log2(math.e)
    own_len, mate_len = ids[0], ids[1]
    for i in range(NSEQ):
        at = slice(BLK * i, BLK * (i + 1))
        q_own[at, :] = own[i, 0:BLK, 0:HEAD]
        k_own[at, :] = own[i, 0:BLK, HEAD : 2 * HEAD]
        q_mate[at, :] = mate[i, 0:BLK, 0:HEAD]
        k_mate[at, :] = mate[i, 0:BLK, HEAD : 2 * HEAD]
        k_t[:, at] = mate[i, 0:BLK, HEAD : 2 * HEAD].astype(F32).T.astype(BF16)
        for n, ref in enumerate((mate, own)):
            ext = ref[i, BLK : BLK + EXT, :].astype(F32)
            row = ext[0:1, 0:BLK] + ext[0:1, BLK : 2 * BLK]
            wcol[n, at, :] = jnp.broadcast_to(row, (BLK, BLK)).T

    def softmax(side, queries, keys, start, key_len):
        q = queries[pl.ds(start, TB), :]
        top = jnp.full((8, TB), -jnp.inf, F32)
        for u in range(NSEQ):
            at = slice(BLK * u, BLK * (u + 1))
            s = lax.dot_general(keys[at, :], q, LAST, preferred_element_type=F32)
            s = s * exponent + jnp.where(u < key_len, 0.0, -1e30).astype(F32)
            scores[at, :] = s
            top = jnp.maximum(top, jnp.max(s.reshape(BLK // 8, 8, TB), axis=0))
        top = jnp.max(top, axis=0, keepdims=True)
        total = jnp.zeros((8, TB), F32)
        weighed = jnp.zeros((8, TB), F32)
        for u in range(2 * NSEQ):
            at = slice(64 * u, 64 * (u + 1))
            e = jnp.exp2(scores[at, :] - top)
            scores[at, :] = e
            w = wcol[side, at, :]
            total += jnp.sum(e.reshape(8, 8, TB), axis=0)
            weighed += jnp.sum((e * jnp.concatenate([w, w], axis=1)).reshape(8, 8, TB), axis=0)
        total = jnp.sum(total, axis=0, keepdims=True)
        inverse = 1.0 / total
        s_row = jnp.sum(weighed, axis=0, keepdims=True) * inverse
        return inverse, s_row

    def live_row(start, length):
        t = lax.broadcasted_iota(jnp.int32, (1, TB), 1) + start
        return jnp.where(t < BLK * length, 1.0, 0.0).astype(F32)

    def first(n, z):
        start = pl.multiple_of(n * TB, TB)
        inverse, s_row = softmax(0, q_own, k_mate, start, mate_len)
        live = live_row(start, own_len)
        for u in range(2 * NSEQ):
            at = slice(64 * u, 64 * (u + 1))
            w = wcol[0, at, :]
            dots[at, :] = (scores[at, :] * (jnp.concatenate([w, w], axis=1) - s_row)).astype(BF16)
        g = jnp.dot(k_t[...], dots[...], preferred_element_type=F32)
        dq[:, pl.ds(start, TB)] = g * (inverse * live)
        return z + s_row * live

    def second(n, z):
        start = pl.multiple_of(n * TB, TB)
        inverse, s_row = softmax(1, q_mate, k_own, start, own_len)
        live = live_row(start, mate_len)
        r = inverse * live
        for u in range(2 * NSEQ):
            at = slice(64 * u, 64 * (u + 1))
            w = wcol[1, at, :]
            f = scores[at, :] * r
            cacc[at, :] += f[:, 0:BLK] + f[:, BLK:TB]
            dots[at, :] = (f * (jnp.concatenate([w, w], axis=1) - s_row)).astype(BF16)
        q = q_mate[pl.ds(start, TB), :]
        dk[...] += jnp.dot(dots[...], q, preferred_element_type=F32)
        return z + s_row * live

    cacc[...] = jnp.zeros_like(cacc)
    dk[...] = jnp.zeros_like(dk)
    zero = jnp.zeros((1, TB), F32)
    z_own = lax.fori_loop(0, SEQLEN // TB, first, zero)
    z_mate = lax.fori_loop(0, SEQLEN // TB, second, zero)

    def head(z_row, length, label, index):
        count = jnp.full((1, 1), BLK * length, jnp.int32).astype(F32)
        sign = jnp.full((1, 1), 2 * label - 1, jnp.int32).astype(F32)
        factor = 32.0 * (1.0 + 2.0 * jnp.full((1, 1), index, jnp.int32).astype(F32) / (NDP - 1))
        root = jnp.sqrt(count)
        x = -sign * (jnp.sum(z_row, axis=1, keepdims=True) / root)
        e = jnp.exp(-jnp.abs(x))
        term = factor * (jnp.maximum(x, 0.0) + jnp.log1p(e))
        sigmoid = jnp.where(x >= 0, 1.0, e) / (1.0 + e)
        return term, -factor * sign * sigmoid / root

    term, ds_own = head(z_own, own_len, ids[2], ids[4])
    _, ds_mate = head(z_mate, mate_len, ids[3], ids[5])
    loss[...] = jnp.broadcast_to(term, (8, BLK))
    row = lax.broadcasted_iota(jnp.int32, (EXT, BLK), 0)
    for i in range(NSEQ):
        at = slice(BLK * i, BLK * (i + 1))
        grads[i, :, 0:HEAD] = (dq[:, at] * (ds_own * scale)).T.astype(BF16)
        grads[i, :, HEAD : 2 * HEAD] = (dk[at, :] * (ds_mate * scale)).astype(BF16)
        c_row = jnp.sum(cacc[at, :].T, axis=0, keepdims=True) * ds_mate
        high, low = halves(c_row)
        crows[i] = jnp.where(row < 2, high, jnp.where(row == 2, low, 0.0)).astype(BF16)


def weight_grads(hidden_t, grads, crows, loss, value_rows, out, ext):
    chunk = 256
    wide = []
    for n in range(COLS // chunk):
        at = slice(chunk * n, chunk * (n + 1))
        acc = jnp.zeros((chunk, 2 * HEAD), F32)
        u = jnp.zeros((EXT, chunk), F32)
        for s in range(NSEQ):
            x = hidden_t[s, at, :]
            acc += jnp.dot(x, grads[s], preferred_element_type=F32)
            u += lax.dot_general(crows[s], x, LAST, preferred_element_type=F32)
        acc = acc.astype(BF16)
        for k in range(chunk // SHARE):
            out[n * (chunk // SHARE) + k, 0:SHARE, :] = acc[SHARE * k : SHARE * (k + 1)]
        wide.append(u[0:1] + u[2:3])
    row = lax.broadcasted_iota(jnp.int32, (EXT, chunk), 0)
    gs = jnp.zeros((EXT, HEAD), F32)
    ext[...] = jnp.zeros_like(ext)
    for n, u in enumerate(wide):
        high, low = halves(u)
        ext[n : n + 1, :] = high
        ext[4 + n : 5 + n, :] = low
        lhs = jnp.where(row == 0, high, jnp.where(row == 1, low, 0.0)).astype(BF16)
        gs += jnp.dot(lhs, value_rows[chunk * n : chunk * (n + 1), :], preferred_element_type=F32)
    high, low = halves(gs[0:1] + gs[1:2])
    ext[8:9, 0:HEAD] = high
    ext[8:9, HEAD : 2 * HEAD] = low
    high, low = halves(loss[0:1, :])
    ext[9:10, 0:HEAD] = high
    ext[9:10, HEAD : 2 * HEAD] = low
    tail = ext[...].astype(BF16)
    for d in range(NDP):
        out[d, SHARE : SHARE + EXT, :] = tail


def sum_shares(received, out, ext):
    acc = received[0].astype(F32)
    for n in range(1, NDP):
        acc += received[n].astype(F32)
    tail = acc[SHARE : SHARE + EXT]
    ext[...] = jnp.zeros_like(ext)
    high, low = halves(tail[0:4] + tail[4:8])
    ext[0:4, :] = high
    ext[4:8, :] = low
    for n in (8, 9):
        high, low = halves(tail[n : n + 1, 0:HEAD] + tail[n : n + 1, HEAD : 2 * HEAD])
        ext[n : n + 1, 0:HEAD] = high
        ext[n : n + 1, HEAD : 2 * HEAD] = low
    rows = acc[0:SHARE].astype(BF16)
    tail = ext[...].astype(BF16)
    for s in range(NSEQ):
        out[s, 0:SHARE, :] = rows
        out[s, SHARE : SHARE + EXT, :] = tail


def unpack(ids, received, score, gq, gk, gv, gs, loss):
    d = ids[0]
    sub = lax.broadcasted_iota(jnp.int32, (4, 2 * HEAD), 0)
    lane = lax.broadcasted_iota(jnp.int32, (SHARE, 2 * HEAD), 1)
    j = lax.broadcasted_iota(jnp.int32, (SHARE, 2 * HEAD), 0)
    hit = lane == SHARE * (d % 8) + j
    readout = jnp.zeros((1, HEAD), F32)
    for s in range(NSEQ):
        at = slice(SHARE * s, SHARE * (s + 1))
        block = received[s].astype(F32)
        gq[at, :] = block[0:SHARE, 0:HEAD]
        gk[at, :] = block[0:SHARE, HEAD : 2 * HEAD]
        tail = block[SHARE : SHARE + EXT]
        u = tail[0:4] + tail[4:8]
        u = jnp.sum(jnp.where(sub == d // 8, u, 0.0), axis=0, keepdims=True)
        column = jnp.sum(jnp.where(hit, u, 0.0), axis=1, keepdims=True)
        gv[at, :] = column * score[...]
        readout += tail[8:9, 0:HEAD] + tail[8:9, HEAD : 2 * HEAD]
        if s == 0:
            loss[...] = tail[9:10, 0:HEAD] + tail[9:10, HEAD : 2 * HEAD]
    gs[...] = readout


def hidden_grads(ids, grads, crows, *refs):
    blocks, out = refs[:-1], refs[-1]
    window = ids[len(blocks)]
    g = grads[window]
    c = crows[window].astype(F32).T.astype(BF16)
    for n, block in enumerate(blocks):
        start = pl.multiple_of(ids[n] * ROWS, ROWS)
        y = lax.dot_general(g, block[0:ROWS, :], LAST, preferred_element_type=F32)
        y += jnp.dot(c, block[ROWS : ROWS + EXT, :], preferred_element_type=F32)
        out[:, pl.ds(start, ROWS)] = y.astype(BF16)


def gather_weights(block):
    swap = [(0, 1), (1, 0)]
    up = [(i, (i + 1) % NZ) for i in range(NZ)]
    down = [(i, (i - 1) % NZ) for i in range(NZ)]
    other = lax.ppermute(block, "xl", swap)
    found = {(0, 0): block, (0, 1): other}
    for step in range(1, NZ // 2 + 1):
        for x in (0, 1):
            if step < NZ // 2 or x == 0:
                found[(-step, x)] = lax.ppermute(found[(1 - step, x)], "z", up)
            if step < NZ // 2 or x == 1:
                found[(step, x)] = lax.ppermute(found[(step - 1, x)], "z", down)
    result = []
    for (dz, dx), piece in found.items():
        result.append(((dz, dx, 0), piece))
        result.append(((dz, dx, 1), lax.ppermute(piece, "c", swap)))
    return result


def per_device(hidden, w_query, w_key, w_value, score_vec, labels, lengths, partner):
    tokens = hidden.reshape(BLK, NDP * ROWS)
    score = score_vec.reshape(1, HEAD)
    z, xl, c = (lax.axis_index(a) for a in DP)
    group = (z * NX + xl) * NC + c
    window = lax.axis_index("y") * 2 + lax.axis_index("xh")
    mate = partner[group]
    swap = [(0, 1), (1, 0)]

    block = call(
        pack_weights, shape((ROWS + EXT, ROWS), BF16), (w_query, w_key, w_value, score), name="pack_weights"
    )
    gathered = gather_weights(block)
    places = [((z + dz) % NZ) * 4 + (xl ^ dx) * 2 + (c ^ dc) for (dz, dx, dc), _ in gathered]
    place_ids = jnp.stack(places + [window]).astype(jnp.int32)
    blocks = [piece for _, piece in gathered]

    split = call(split_columns, shape((NSEQ, COLS, BLK), BF16), (tokens,), name="split_columns", flops=1 << 30)
    hidden_t = lax.all_to_all(split, SEQ, 0, 0, tiled=True)
    own_rows = lax.dynamic_slice_in_dim(w_value, window * SHARE, SHARE, 0)
    value_rows = lax.all_gather(own_rows, DP, axis=0, tiled=True)

    payload = call(
        project,
        shape((NSEQ, BLK + EXT, 2 * HEAD), BF16),
        (place_ids, tokens, *blocks),
        name="project",
        flops=1 << 29,
        bytes_accessed=6 << 20,
    )
    own = lax.all_to_all(payload, SEQ, 0, 0, tiled=True)
    mine = payload[0]
    core = lax.ppermute(mine, "c", swap)
    side = lax.ppermute(mine, "xl", swap)
    both = lax.ppermute(core, "xl", swap)
    here = xl * 2 + c
    wanted = (partner[jnp.arange(NZ) * 4 + here] % 4) ^ here
    slots = call(
        pick_for_planes,
        shape((NZ, BLK + EXT, 2 * HEAD), BF16),
        (wanted.astype(jnp.int32), mine, core, side, both),
        scratch=[pltpu.VMEM((4, BLK + EXT, 2 * HEAD), BF16)],
        name="pick_for_planes",
    )
    arrived = lax.all_to_all(slots, "z", 0, 0, tiled=True)
    theirs = call(
        pick_partner,
        shape((NSEQ, BLK + EXT, 2 * HEAD), BF16),
        ((mate // 4).reshape(1).astype(jnp.int32), arrived),
        name="pick_partner",
    )
    other = lax.all_to_all(theirs, SEQ, 0, 0, tiled=True)

    heads = jnp.stack([lengths[group], lengths[mate], labels[group], labels[mate], group, mate]).astype(jnp.int32)
    grads, crows, term = call(
        attention,
        (shape((NSEQ, BLK, 2 * HEAD), BF16), shape((NSEQ, EXT, BLK), BF16), shape((8, BLK), F32)),
        (heads, own, other),
        scratch=[
            pltpu.VMEM((HEAD, SEQLEN), BF16),
            pltpu.VMEM((HEAD, SEQLEN), BF16),
            pltpu.VMEM((SEQLEN, HEAD), BF16),
            pltpu.VMEM((SEQLEN, HEAD), BF16),
            pltpu.VMEM((SEQLEN, HEAD), BF16),
            pltpu.VMEM((SEQLEN, HEAD), BF16),
            pltpu.VMEM((2, SEQLEN, BLK), F32),
            pltpu.VMEM((SEQLEN, TB), F32),
            pltpu.VMEM((SEQLEN, TB), BF16),
            pltpu.VMEM((HEAD, SEQLEN), F32),
            pltpu.VMEM((SEQLEN, HEAD), F32),
            pltpu.VMEM((SEQLEN, BLK), F32),
        ],
        name="attention",
        flops=1 << 31,
    )
    shares = call(
        weight_grads,
        shape((NDP, SHARE + EXT, 2 * HEAD), BF16),
        (hidden_t, grads, crows, term, value_rows),
        scratch=[pltpu.VMEM((EXT, 2 * HEAD), F32)],
        name="weight_grads",
        flops=1 << 29,
    )
    arrived = lax.all_to_all(shares, DP, 0, 0, tiled=True)
    grad_hidden = call(
        hidden_grads,
        shape((BLK, NDP * ROWS), BF16),
        (place_ids, grads, crows, *blocks),
        name="hidden_grads",
        flops=1 << 29,
        bytes_accessed=6 << 20,
    )
    sums = call(
        sum_shares,
        shape((NSEQ, SHARE + EXT, 2 * HEAD), BF16),
        (arrived,),
        scratch=[pltpu.VMEM((EXT, 2 * HEAD), F32)],
        name="sum_shares",
    )
    arrived = lax.all_to_all(sums, SEQ, 0, 0, tiled=True)
    grad_query, grad_key, grad_value, grad_score, loss = call(
        unpack,
        (
            shape((ROWS, HEAD), F32),
            shape((ROWS, HEAD), F32),
            shape((ROWS, HEAD), F32),
            shape((1, HEAD), F32),
            shape((1, HEAD), F32),
        ),
        (group.reshape(1).astype(jnp.int32), arrived, score),
        name="unpack",
    )
    return (
        loss[0, 0],
        grad_query,
        grad_key,
        grad_value,
        grad_score.reshape(HEAD),
        grad_hidden.reshape(1, BLK, NDP * ROWS),
    )


def solution(mesh):
    parts = Mesh(mesh.devices.reshape(NZ, NX, NC, 4, 2), DP + SEQ)
    return jax.shard_map(
        per_device,
        mesh=parts,
        in_specs=(P(DP, SEQ, None), P(DP, None), P(DP, None), P(DP, None), P(), P(), P(), P()),
        out_specs=(P(), P(DP, None), P(DP, None), P(DP, None), P(), P(DP, SEQ, None)),
        check_vma=False,
    )
```

```python
import functools
import math

import jax
import jax.numpy as jnp
from jax import lax
from jax.experimental import pallas as pl
from jax.experimental.pallas import tpu as pltpu
from jax.sharding import Mesh
from jax.sharding import PartitionSpec as P

F32 = jnp.float32
BF16 = jnp.bfloat16
NZ, NX, NC = 8, 2, 2
NDP = NZ * NX * NC
NSEQ = 8
BLK = 128
HEAD = 128
ROWS = 256
EXT = 16
BLOCK = ROWS + 2 * EXT
SHARE = ROWS // NSEQ
COLS = NDP * SHARE
SEQLEN = NSEQ * BLK
TB = 256
DP = ("z", "xl", "c")
SEQ = ("y", "xh")
LAST = (((1,), (1,)), ((), ()))
VM = pl.BlockSpec(memory_space=pltpu.VMEM)
SM = pl.BlockSpec(memory_space=pltpu.SMEM)
HBM = pl.BlockSpec(memory_space=pltpu.HBM)
WINDOW, GROUP, WANTED, MATE_STEP, HEADS, CORE = 16, 17, 18, 26, 27, 33


def call(kernel, outs, ins, scratch=(), far=(), far_out=(), flops=0, bytes_accessed=0, name=None, limit=48):
    return pl.pallas_call(
        kernel,
        out_shape=outs,
        in_specs=[SM if a.dtype == jnp.int32 else HBM if n in far else VM for n, a in enumerate(ins)],
        out_specs=jax.tree.map(lambda o: SM if o.dtype == jnp.int32 else HBM if o.shape in far_out else VM, outs),
        scratch_shapes=list(scratch),
        compiler_params=pltpu.CompilerParams(vmem_limit_bytes=limit * 1024 * 1024),
        cost_estimate=pl.CostEstimate(flops=flops, bytes_accessed=bytes_accessed, transcendentals=0),
        name=name,
    )(*ins)


def shape(dims, dtype):
    return jax.ShapeDtypeStruct(dims, dtype)


def halves(x):
    high = x.astype(BF16).astype(F32)
    return high, x - high


def pack_weights(pos, lengths, labels, partner, wq, wk, wv, score, out, ids, wvs, sems):
    copies = [
        pltpu.make_async_copy(wq, out.at[0:ROWS, 0:HEAD], sems.at[0]),
        pltpu.make_async_copy(wk, out.at[0:ROWS, HEAD : 2 * HEAD], sems.at[1]),
        pltpu.make_async_copy(wv, wvs, sems.at[2]),
    ]
    for copy in copies:
        copy.start()
    z, xl, c, window = pos[0], pos[1], pos[2], pos[3]
    here = xl * 2 + c
    for n, (dz, dx) in enumerate(ORDER):
        ids[n] = ((z + dz + NZ) % NZ) * 4 + (xl ^ dx) * 2 + c
    group = z * 4 + here
    mate = partner[group]
    ids[WINDOW] = window
    ids[GROUP] = group
    for k in range(NZ):
        ids[WANTED + k] = (partner[((z + k) % NZ) * 4 + here] & 3) ^ here
    ids[MATE_STEP] = (z - (mate >> 2) + NZ) % NZ
    for n, x in enumerate((lengths[group], lengths[mate], labels[group], labels[mate], group, mate)):
        ids[HEADS + n] = x
    ids[CORE] = c
    for copy in copies:
        copy.wait()
    s1, rest = halves(score[...])
    s2, s3 = halves(rest)
    row = lax.broadcasted_iota(jnp.int32, (EXT, HEAD), 0)
    lhs = jnp.where(row == 0, s1, jnp.where(row == 1, s2, jnp.where(row == 2, s3, 0.0)))
    product = lax.dot_general(lhs.astype(BF16), wvs[...], LAST, preferred_element_type=F32)
    total = jnp.sum(product, axis=0, keepdims=True)
    high, low = halves(total)
    row = lax.broadcasted_iota(jnp.int32, (EXT, ROWS), 0)
    ext = jnp.where((row == 0) | (row == 2), high, jnp.where(row == 1, low, 0.0))
    out[ROWS : ROWS + EXT, :] = ext.astype(BF16)
    for h in range(2):
        start = pl.multiple_of(window * SHARE + EXT * h, EXT)
        out[ROWS + EXT : BLOCK, HEAD * h : HEAD * (h + 1)] = wvs[pl.ds(start, EXT), :]


def split_columns(hidden, out):
    size, many = 4 * BLK, 4
    i = lax.broadcasted_iota(jnp.int32, (size, size), 0)
    o = lax.broadcasted_iota(jnp.int32, (size, size), 1)
    source = BLK * ((o & 127) >> 5) + SHARE * (o >> 7) + (o & 31)
    perm = jnp.where(i == source, 1.0, 0.0).astype(BF16)
    for h in range(2):
        for first in range(0, NDP // 4, many):
            x = [
                jnp.concatenate([hidden[:, ROWS * (4 * q + k) + BLK * h :][:, :BLK] for k in range(4)], axis=1)
                for q in range(first, first + many)
            ]
            y = jnp.dot(jnp.concatenate(x, axis=0), perm, preferred_element_type=F32).astype(BF16)
            for k in range(many):
                for r in range(4):
                    out[4 * h + r, :, BLK * (first + k) : BLK * (first + k + 1)] = y[BLK * k :][:BLK, BLK * r :][:, :BLK]


def project(ids, hidden, sibling, *refs):
    blocks, (out, kept, x, w, exts, sems, out_sems) = refs[:-7], refs[-7:]
    arrivals, leaving = [], []
    for n, block in enumerate(blocks):
        columns = pl.ds(pl.multiple_of(ids[n] * ROWS, ROWS), ROWS)
        at = slice(ROWS * n, ROWS * (n + 1))
        pairs = (
            (block.at[0:ROWS], w.at[at]),
            (block.at[ROWS:BLOCK], exts.at[n]),
            (hidden.at[:, columns], x.at[0:BLK, at]),
            (sibling.at[:, columns], x.at[BLK : 2 * BLK, at]),
        )
        arrivals.append([pltpu.make_async_copy(a, b, sems.at[n, i]) for i, (a, b) in enumerate(pairs)])
        leaving.append(pltpu.make_async_copy(w.at[at], kept.at[n, 0:ROWS], out_sems.at[n, 0]))
        leaving.append(pltpu.make_async_copy(exts.at[n], kept.at[n, ROWS:BLOCK], out_sems.at[n, 1]))
    for group in arrivals:
        for copy in group:
            copy.start()
    acc = jnp.zeros((2 * BLK, 2 * HEAD), F32)
    wide = [jnp.zeros((BLK, BLK), F32)] * 2
    many = 4
    for first in range(0, len(blocks), many):
        for n in range(first, first + many):
            for copy in arrivals[n]:
                copy.wait()
            leaving[2 * n].start()
            leaving[2 * n + 1].start()
        at = slice(ROWS * first, ROWS * (first + many))
        acc += jnp.dot(x[:, at], w[at, :], preferred_element_type=F32)
        for n in range(first, first + many):
            ext = exts[n, 0:EXT, :].astype(F32)
            row = ext[0:1] + ext[1:2]
            for m in range(2):
                product = x[BLK * m : BLK * (m + 1), ROWS * n : ROWS * (n + 1)].astype(F32) * row
                wide[m] += product[:, 0:BLK] + product[:, BLK : 2 * BLK]
    zeros = jnp.zeros((8, 2 * HEAD), F32)
    for m in range(2):
        total = jnp.sum(wide[m].T, axis=0, keepdims=True)
        out[m, 0:BLK, :] = acc[BLK * m : BLK * (m + 1)]
        out[m, BLK : BLK + 8, :] = zeros + jnp.concatenate([total, total], axis=1)
    for copy in leaving:
        copy.wait()


def join_cores(mine, theirs, items):
    row = lax.broadcasted_iota(jnp.int32, (EXT, 2 * HEAD), 0)
    for n in range(2):
        full = mine[n] + theirs[1 - n]
        high, low = halves(full[BLK : BLK + 1, 0:BLK])
        items[n, 0:BLK, :] = full[0:BLK].astype(BF16)
        items[n, BLK : BLK + EXT, :] = jnp.where(row == 0, jnp.concatenate([high, low], axis=1), 0.0).astype(BF16)


def repeat_own(items, out, sems):
    copies = [pltpu.make_async_copy(items.at[0], out.at[s], sems.at[s]) for s in range(NSEQ)]
    for copy in copies:
        copy.start()
    for copy in copies:
        copy.wait()


def pick_for_planes(ids, near, side, *refs):
    outs, items = refs[:-1], refs[-1]
    items[0:2] = near[...]
    items[2:4] = side[...]
    for k, out in enumerate(outs):
        out[...] = items[ids[WANTED + k]]


def pick_partner(ids, *refs):
    received, (out, mine, sem, sems) = refs[:-4], refs[-4:]
    for k, ref in enumerate(received):

        @pl.when(ids[MATE_STEP] == k)
        def _(ref=ref):
            copy = pltpu.make_async_copy(ref, mine, sem.at[0])
            copy.start()
            copy.wait()

    copies = [pltpu.make_async_copy(mine, out.at[s], sems.at[s]) for s in range(NSEQ)]
    for copy in copies:
        copy.start()
    for copy in copies:
        copy.wait()


def collect_values(ids, kept, swapped, out, rows, sems):
    copies = [
        pltpu.make_async_copy(ref.at[:, ROWS + EXT : BLOCK, :], rows.at[n], sems.at[n])
        for n, ref in enumerate((kept, swapped))
    ]
    for copy in copies:
        copy.start()
    for flip, copy in enumerate(copies):
        copy.wait()
        for n in range(len(ORDER)):
            d = ids[n] ^ flip
            for h in range(2):
                start = pl.multiple_of(d * SHARE + EXT * h, EXT)
                out[pl.ds(start, EXT), :] = rows[flip, n, :, HEAD * h : HEAD * (h + 1)]


def attention(
    ids,
    own,
    mate,
    hidden,
    values,
    keep,
    send,
    grads,
    crows,
    exts,
    k_t,
    q_own,
    k_own,
    q_mate,
    k_mate,
    wcol,
    scores,
    dots,
    dq,
    dk,
    cacc,
    all_grads,
    columns,
    value_rows,
    shares,
    ext,
    sems,
    late_sems,
):
    copies = []
    for n, (ref, q, k) in enumerate(((mate, q_mate, k_mate), (own, q_own, k_own))):
        copies.append(pltpu.make_async_copy(ref.at[:, 0:BLK, 0:HEAD], q, sems.at[3 * n]))
        copies.append(pltpu.make_async_copy(ref.at[:, 0:BLK, HEAD : 2 * HEAD], k, sems.at[3 * n + 1]))
        copies.append(pltpu.make_async_copy(ref.at[:, BLK : BLK + EXT, :], exts.at[n], sems.at[3 * n + 2]))
    for copy in copies:
        copy.start()
    late = [
        pltpu.make_async_copy(hidden, columns, late_sems.at[0]),
        pltpu.make_async_copy(values, value_rows, late_sems.at[1]),
    ]
    for copy in late:
        copy.start()
    cacc[...] = jnp.zeros_like(cacc)
    dk[...] = jnp.zeros_like(dk)
    for copy in copies:
        copy.wait()
    scale = 1.0 / math.sqrt(HEAD)
    exponent = scale * math.log2(math.e)
    own_len, mate_len = ids[HEADS], ids[HEADS + 1]
    for i in range(NSEQ):
        at = slice(BLK * i, BLK * (i + 1))
        k_t[:, at] = k_mate[i].astype(F32).T.astype(BF16)
        for n in range(2):
            extra = exts[n, i].astype(F32)
            row = extra[0:1, 0:BLK] + extra[0:1, BLK : 2 * BLK]
            wcol[n, at, :] = jnp.broadcast_to(row, (BLK, BLK)).T

    def softmax(side, queries, keys, start, key_len):
        q = queries[pl.ds(start // BLK, TB // BLK)].reshape(TB, HEAD)
        top = jnp.full((8, TB), -jnp.inf, F32)
        for u in range(NSEQ):
            at = slice(BLK * u, BLK * (u + 1))
            s = lax.dot_general(keys[u], q, LAST, preferred_element_type=F32)
            s = s * exponent + jnp.where(u < key_len, 0.0, -1e30).astype(F32)
            scores[side, at, :] = s
            top = jnp.maximum(top, jnp.max(s.reshape(BLK // 8, 8, TB), axis=0))
        top = jnp.max(top, axis=0, keepdims=True)
        total = jnp.zeros((8, TB), F32)
        weighed = jnp.zeros((8, TB), F32)
        for u in range(2 * NSEQ):
            at = slice(64 * u, 64 * (u + 1))
            e = jnp.exp2(scores[side, at, :] - top)
            scores[side, at, :] = e
            w = wcol[side, at, :]
            total += jnp.sum(e.reshape(8, 8, TB), axis=0)
            weighed += jnp.sum((e * jnp.concatenate([w, w], axis=1)).reshape(8, 8, TB), axis=0)
        total = jnp.sum(total, axis=0, keepdims=True)
        inverse = 1.0 / total
        s_row = jnp.sum(weighed, axis=0, keepdims=True) * inverse
        return inverse, s_row

    def live_row(start, length):
        t = lax.broadcasted_iota(jnp.int32, (1, TB), 1) + start
        return jnp.where(t < BLK * length, 1.0, 0.0).astype(F32)

    def first(n, z):
        side = 0
        start = pl.multiple_of(n * TB, TB)
        inverse, s_row = softmax(0, q_own, k_mate, start, mate_len)
        live = live_row(start, own_len)
        for u in range(2 * NSEQ):
            at = slice(64 * u, 64 * (u + 1))
            w = wcol[0, at, :]
            dots[side, at, :] = (scores[side, at, :] * (jnp.concatenate([w, w], axis=1) - s_row)).astype(BF16)
        g = jnp.dot(k_t[...], dots[side], preferred_element_type=F32)
        dq[:, pl.ds(start, TB)] = g * (inverse * live)
        return z + s_row * live

    def second(n, z):
        side = 1
        start = pl.multiple_of(n * TB, TB)
        inverse, s_row = softmax(1, q_mate, k_own, start, own_len)
        live = live_row(start, mate_len)
        r = inverse * live
        for u in range(2 * NSEQ):
            at = slice(64 * u, 64 * (u + 1))
            w = wcol[1, at, :]
            f = scores[side, at, :] * r
            cacc[at, :] += f[:, 0:BLK] + f[:, BLK:TB]
            dots[side, at, :] = (f * (jnp.concatenate([w, w], axis=1) - s_row)).astype(BF16)
        q = q_mate[pl.ds(start // BLK, TB // BLK)].reshape(TB, HEAD)
        dk[...] += jnp.dot(dots[side], q, preferred_element_type=F32)
        return z + s_row * live

    zero = jnp.zeros((1, TB), F32)

    def both(n, z):
        return first(n, z[0]), second(n, z[1])

    z_own, z_mate = lax.fori_loop(0, SEQLEN // TB, both, (zero, zero))

    def head(z_row, length, label, index):
        count = jnp.full((1, 1), BLK * length, jnp.int32).astype(F32)
        sign = jnp.full((1, 1), 2 * label - 1, jnp.int32).astype(F32)
        factor = 32.0 * (1.0 + 2.0 * jnp.full((1, 1), index, jnp.int32).astype(F32) / (NDP - 1))
        root = jnp.sqrt(count)
        x = -sign * (jnp.sum(z_row, axis=1, keepdims=True) / root)
        e = jnp.exp(-jnp.abs(x))
        term = factor * (jnp.maximum(x, 0.0) + jnp.log1p(e))
        sigmoid = jnp.where(x >= 0, 1.0, e) / (1.0 + e)
        return term, -factor * sign * sigmoid / root

    term, ds_own = head(z_own, own_len, ids[HEADS + 2], ids[HEADS + 4])
    _, ds_mate = head(z_mate, mate_len, ids[HEADS + 3], ids[HEADS + 5])
    row = lax.broadcasted_iota(jnp.int32, (EXT, BLK), 0)
    for i in range(NSEQ):
        at = slice(BLK * i, BLK * (i + 1))
        all_grads[0:HEAD, at] = (dq[:, at] * (ds_own * scale)).astype(BF16)
        all_grads[HEAD : 2 * HEAD, at] = (dk[at, :] * (ds_mate * scale)).T.astype(BF16)
        c_row = jnp.sum(cacc[at, :].T, axis=0, keepdims=True) * ds_mate
        high, low = halves(c_row)
        c_rows = jnp.where(row < 2, high, jnp.where(row == 2, low, 0.0)).astype(BF16)
        all_grads[2 * HEAD : 2 * HEAD + EXT, at] = c_rows

        @pl.when(ids[WINDOW] == i)
        def _(at=at, c_rows=c_rows):
            grads[...] = all_grads[0 : 2 * HEAD, at].astype(F32).T.astype(BF16)
            crows[...] = c_rows

    for copy in late:
        copy.wait()
    chunk = 256
    wide = []
    for n in range(COLS // chunk):
        x = columns[:, :, chunk * n : chunk * (n + 1)].reshape(SEQLEN, chunk)
        y = jnp.dot(all_grads[...], x, preferred_element_type=F32)
        rows = y[0 : 2 * HEAD].T
        for k in range(chunk // SHARE):
            d = n * (chunk // SHARE) + k
            shares[(d & 1) ^ ids[CORE], d >> 1] = rows[SHARE * k : SHARE * (k + 1)]
        wide.append(y[2 * HEAD : 2 * HEAD + 1] + y[2 * HEAD + 2 : 2 * HEAD + 3])
    row = lax.broadcasted_iota(jnp.int32, (EXT, chunk), 0)
    gs = jnp.zeros((EXT, HEAD), F32)
    ext[...] = jnp.zeros_like(ext)
    for n, u in enumerate(wide):
        high, low = halves(u)
        ext[n : n + 1, :] = high
        ext[4 + n : 5 + n, :] = low
        lhs = jnp.where(row == 0, high, jnp.where(row == 1, low, 0.0)).astype(BF16)
        gs += jnp.dot(lhs, value_rows[chunk * n : chunk * (n + 1), :], preferred_element_type=F32)
    high, low = halves(gs[0:1] + gs[1:2])
    ext[8:9, 0:HEAD] = high
    ext[8:9, HEAD : 2 * HEAD] = low
    high, low = halves(jnp.broadcast_to(term, (1, HEAD)))
    ext[9:10, 0:HEAD] = high
    ext[9:10, HEAD : 2 * HEAD] = low
    tail = ext[...]
    for m in range(NDP // 2):
        keep[m, 0:SHARE, :] = shares[0, m]
        keep[m, SHARE : SHARE + EXT, :] = tail
        send[m, 0:SHARE, :] = shares[1, m].astype(BF16)
        send[m, SHARE : SHARE + EXT, :] = tail.astype(BF16)


def add_core(keep, received, out, ext):
    split_again(keep[0, SHARE : SHARE + EXT, :] + received[0, SHARE : SHARE + EXT, :].astype(F32), ext)
    tail = ext[...].astype(BF16)
    for m in range(NDP // 2):
        out[m, 0:SHARE, :] = (keep[m, 0:SHARE, :] + received[m, 0:SHARE, :].astype(F32)).astype(BF16)
        out[m, SHARE : SHARE + EXT, :] = tail


def split_again(tail, ext):
    ext[...] = jnp.zeros_like(ext)
    high, low = halves(tail[0:4] + tail[4:8])
    ext[0:4, :] = high
    ext[4:8, :] = low
    for n in (8, 9):
        high, low = halves(tail[n : n + 1, 0:HEAD] + tail[n : n + 1, HEAD : 2 * HEAD])
        ext[n : n + 1, 0:HEAD] = high
        ext[n : n + 1, HEAD : 2 * HEAD] = low


def sum_shares(received, out, ext):
    acc = received[0].astype(F32)
    for n in range(1, NDP // 2):
        acc += received[n].astype(F32)
    split_again(acc[SHARE : SHARE + EXT], ext)
    rows = acc[0:SHARE].astype(BF16)
    tail = ext[...].astype(BF16)
    for s in range(NSEQ):
        out[s, 0:SHARE, :] = rows
        out[s, SHARE : SHARE + EXT, :] = tail


def unpack(ids, received, score, gq, gk, gv, gs, loss):
    d = ids[GROUP]
    sub = lax.broadcasted_iota(jnp.int32, (4, 2 * HEAD), 0)
    lane = lax.broadcasted_iota(jnp.int32, (SHARE, 2 * HEAD), 1)
    j = lax.broadcasted_iota(jnp.int32, (SHARE, 2 * HEAD), 0)
    hit = lane == SHARE * (d % 8) + j
    readout = jnp.zeros((1, HEAD), F32)
    for s in range(NSEQ):
        at = slice(SHARE * s, SHARE * (s + 1))
        block = received[s].astype(F32)
        gq[at, :] = block[0:SHARE, 0:HEAD]
        gk[at, :] = block[0:SHARE, HEAD : 2 * HEAD]
        tail = block[SHARE : SHARE + EXT]
        u = tail[0:4] + tail[4:8]
        u = jnp.sum(jnp.where(sub == d // 8, u, 0.0), axis=0, keepdims=True)
        column = jnp.sum(jnp.where(hit, u, 0.0), axis=1, keepdims=True)
        gv[at, :] = column * score[...]
        readout += tail[8:9, 0:HEAD] + tail[8:9, HEAD : 2 * HEAD]
        if s == 0:
            loss[...] = tail[9:10, 0:HEAD] + tail[9:10, HEAD : 2 * HEAD]
    gs[...] = readout


def hidden_grads(ids, grads, crows, kept, swapped, out):
    g = grads[...]
    c = crows[...].astype(F32).T.astype(BF16)
    for flip, ref in enumerate((kept, swapped)):
        for n in range(len(ORDER)):
            start = pl.multiple_of((ids[n] ^ flip) * ROWS, ROWS)
            y = lax.dot_general(g, ref[n, 0:ROWS, :], LAST, preferred_element_type=F32)
            y += jnp.dot(c, ref[n, ROWS : ROWS + EXT, :], preferred_element_type=F32)
            out[:, pl.ds(start, ROWS)] = y.astype(BF16)


SWAP = [(0, 1), (1, 0)]
UP = [(i, (i + 1) % NZ) for i in range(NZ)]
DOWN = [(i, (i - 1) % NZ) for i in range(NZ)]
ORDER = [(0, 0), (0, 1)]
for _step in range(1, NZ // 2 + 1):
    for _x in (0, 1):
        if _step < NZ // 2 or _x == 0:
            ORDER.append((-_step, _x))
        if _step < NZ // 2 or _x == 1:
            ORDER.append((_step, _x))


def gather_weights(block, other, up, down):
    found = {(0, 0): block, (0, 1): other, (-1, 0): up, (1, 0): down}
    for dz, dx in ORDER[2:]:
        if (dz, dx) in found:
            continue
        if dz < 0:
            found[(dz, dx)] = lax.ppermute(found[(dz + 1, dx)], "z", UP)
        else:
            found[(dz, dx)] = lax.ppermute(found[(dz - 1, dx)], "z", DOWN)
    return [found[key] for key in ORDER]


def per_device(hidden, w_query, w_key, w_value, score_vec, labels, lengths, partner):
    tokens = hidden.reshape(BLK, NDP * ROWS)
    score = score_vec.reshape(1, HEAD)
    z, xl, c = (lax.axis_index(a) for a in DP)
    window = lax.axis_index("y") * 2 + lax.axis_index("xh")
    pos = jnp.stack([z, xl, c, window]).astype(jnp.int32)
    item = (BLK + EXT, 2 * HEAD)

    block, ids = call(
        pack_weights,
        (shape((BLOCK, ROWS), BF16), shape((64,), jnp.int32)),
        (pos, lengths, labels, partner, w_query, w_key, w_value, score),
        far=(4, 5, 6),
        scratch=[pltpu.VMEM((ROWS, HEAD), BF16), pltpu.SemaphoreType.DMA((3,))],
        name="pack_weights",
        limit=62,
    )
    other = lax.ppermute(block, "xl", SWAP)
    sibling = lax.ppermute(tokens, "c", SWAP)
    up = lax.ppermute(block, "z", UP)
    down = lax.ppermute(block, "z", DOWN)
    later, _ = lax.optimization_barrier((tokens, block))
    split = call(split_columns, shape((NSEQ, BLK, COLS), BF16), (later,), name="split_columns", flops=1 << 30)
    other, split = lax.optimization_barrier((other, split))
    hidden_t = lax.all_to_all(split, SEQ, 0, 0, tiled=True)
    blocks = gather_weights(block, other, up, down)

    partial, kept = call(
        project,
        (shape((2, BLK + 8, 2 * HEAD), F32), shape((len(ORDER), BLOCK, ROWS), BF16)),
        (ids, tokens, sibling, *blocks),
        far=range(1, 3 + len(ORDER)),
        far_out=((len(ORDER), BLOCK, ROWS),),
        scratch=[
            pltpu.VMEM((2 * BLK, len(ORDER) * ROWS), BF16),
            pltpu.VMEM((len(ORDER) * ROWS, ROWS), BF16),
            pltpu.VMEM((len(ORDER), 2 * EXT, ROWS), BF16),
            pltpu.SemaphoreType.DMA((len(ORDER), 4)),
            pltpu.SemaphoreType.DMA((len(ORDER), 2)),
        ],
        name="project",
        limit=62,
        flops=1 << 29,
        bytes_accessed=6 << 20,
    )
    theirs = lax.ppermute(partial, "c", SWAP)
    theirs, hidden_t = lax.optimization_barrier((theirs, hidden_t))
    items = call(join_cores, shape((2, *item), BF16), (partial, theirs), name="join_cores")
    side = lax.ppermute(items, "xl", SWAP)
    repeated = call(
        repeat_own,
        shape((NSEQ, *item), BF16),
        (items,),
        far_out=((NSEQ, *item),),
        scratch=[pltpu.SemaphoreType.DMA((NSEQ,))],
        name="repeat_own",
    )
    side, repeated = lax.optimization_barrier((side, repeated))
    own = lax.all_to_all(repeated, SEQ, 0, 0, tiled=True)
    slots = call(
        pick_for_planes,
        tuple(shape(item, BF16) for _ in range(NZ)),
        (ids, items, side),
        scratch=[pltpu.VMEM((4, *item), BF16)],
        name="pick_for_planes",
    )
    arrived = {0: slots[0]}
    for k in (4, 3, 5, 2, 6, 1, 7):
        arrived[k] = lax.ppermute(slots[k], "z", [(i, (i + k) % NZ) for i in range(NZ)])
    kept, _ = lax.optimization_barrier((kept, slots[0]))
    swapped = lax.ppermute(kept, "c", SWAP)
    values = call(
        collect_values,
        shape((COLS, HEAD), BF16),
        (ids, kept, swapped),
        far=(1, 2),
        scratch=[pltpu.VMEM((2, len(ORDER), EXT, ROWS), BF16), pltpu.SemaphoreType.DMA((2,))],
        name="collect_values",
        limit=62,
    )
    theirs = call(
        pick_partner,
        shape((NSEQ, *item), BF16),
        (ids, *[arrived[k] for k in range(NZ)]),
        far=range(1, 1 + NZ),
        far_out=((NSEQ, *item),),
        scratch=[pltpu.VMEM(item, BF16), pltpu.SemaphoreType.DMA((1,)), pltpu.SemaphoreType.DMA((NSEQ,))],
        name="pick_partner",
        limit=62,
    )
    theirs, values = lax.optimization_barrier((theirs, values))
    mate = lax.all_to_all(theirs, SEQ, 0, 0, tiled=True)

    message = (NDP // 2, SHARE + EXT, 2 * HEAD)
    ext = pltpu.VMEM((EXT, 2 * HEAD), F32)
    keep, send, grads, crows = call(
        attention,
        (shape(message, F32), shape(message, BF16), shape((BLK, 2 * HEAD), BF16), shape((EXT, BLK), BF16)),
        (ids, own, mate, hidden_t, values),
        far=(1, 2, 3, 4),
        scratch=[
            pltpu.VMEM((2, NSEQ, EXT, 2 * HEAD), BF16),
            pltpu.VMEM((HEAD, SEQLEN), BF16),
            *[pltpu.VMEM((NSEQ, BLK, HEAD), BF16)] * 4,
            pltpu.VMEM((2, SEQLEN, BLK), F32),
            pltpu.VMEM((2, SEQLEN, TB), F32),
            pltpu.VMEM((2, SEQLEN, TB), BF16),
            pltpu.VMEM((HEAD, SEQLEN), F32),
            pltpu.VMEM((SEQLEN, HEAD), F32),
            pltpu.VMEM((SEQLEN, BLK), F32),
            pltpu.VMEM((2 * HEAD + EXT, SEQLEN), BF16),
            pltpu.VMEM((NSEQ, BLK, COLS), BF16),
            pltpu.VMEM((COLS, HEAD), BF16),
            pltpu.VMEM((2, NDP // 2, SHARE, 2 * HEAD), F32),
            ext,
            pltpu.SemaphoreType.DMA((6,)),
            pltpu.SemaphoreType.DMA((2,)),
        ],
        name="attention",
        limit=62,
        flops=1 << 31,
    )
    shares = call(add_core, shape(message, BF16), (keep, lax.ppermute(send, "c", SWAP)), scratch=[ext], name="add_core")
    arrived = lax.all_to_all(shares, ("z", "xl"), 0, 0, tiled=True)
    grad_hidden = call(
        hidden_grads,
        shape((BLK, NDP * ROWS), BF16),
        (ids, grads, crows, kept, swapped),
        name="hidden_grads",
        flops=1 << 29,
        bytes_accessed=6 << 20,
    )
    arrived, grad_hidden = lax.optimization_barrier((arrived, grad_hidden))
    sums = call(
        sum_shares,
        shape((NSEQ, SHARE + EXT, 2 * HEAD), BF16),
        (arrived,),
        scratch=[ext],
        name="sum_shares",
    )
    arrived = lax.all_to_all(sums, SEQ, 0, 0, tiled=True)
    grad_query, grad_key, grad_value, grad_score, loss = call(
        unpack,
        (
            shape((ROWS, HEAD), F32),
            shape((ROWS, HEAD), F32),
            shape((ROWS, HEAD), F32),
            shape((1, HEAD), F32),
            shape((1, HEAD), F32),
        ),
        (ids, arrived, score),
        name="unpack",
    )
    return (
        loss[0, 0],
        grad_query,
        grad_key,
        grad_value,
        grad_score.reshape(HEAD),
        grad_hidden.reshape(1, BLK, NDP * ROWS),
    )


def solution(mesh):
    parts = Mesh(mesh.devices.reshape(NZ, NX, NC, 4, 2), DP + SEQ)
    return jax.shard_map(
        per_device,
        mesh=parts,
        in_specs=(P(DP, SEQ, None), P(DP, None), P(DP, None), P(DP, None), P(), P(), P(), P()),
        out_specs=(P(), P(DP, None), P(DP, None), P(DP, None), P(), P(DP, SEQ, None)),
        check_vma=False,
    )
```

```python
import functools
import math

import jax
import jax.numpy as jnp
from jax import lax
from jax.experimental import pallas as pl
from jax.experimental.pallas import tpu as pltpu
from jax.sharding import Mesh
from jax.sharding import PartitionSpec as P

F32 = jnp.float32
BF16 = jnp.bfloat16
NZ, NX, NC = 8, 2, 2
NDP = NZ * NX * NC
NSEQ = 8
BLK = 128
HEAD = 128
ROWS = 256
EXT = 16
BLOCK = ROWS + 2 * EXT
SHARE = ROWS // NSEQ
COLS = NDP * SHARE
SEQLEN = NSEQ * BLK
TB = 256
DP = ("z", "xl", "c")
SEQ = ("y", "xh")
LAST = (((1,), (1,)), ((), ()))
VM = pl.BlockSpec(memory_space=pltpu.VMEM)
SM = pl.BlockSpec(memory_space=pltpu.SMEM)
HBM = pl.BlockSpec(memory_space=pltpu.HBM)
WINDOW, GROUP, WANTED, MATE_STEP, HEADS, CORE, OWN = 16, 17, 18, 26, 27, 33, 34


def call(kernel, outs, ins, scratch=(), far=(), far_out=(), flops=0, bytes_accessed=0, name=None, limit=48):
    return pl.pallas_call(
        kernel,
        out_shape=outs,
        in_specs=[SM if a.dtype == jnp.int32 else HBM if n in far else VM for n, a in enumerate(ins)],
        out_specs=jax.tree.map(lambda o: SM if o.dtype == jnp.int32 else HBM if o.shape in far_out else VM, outs),
        scratch_shapes=list(scratch),
        compiler_params=pltpu.CompilerParams(vmem_limit_bytes=limit * 1024 * 1024),
        cost_estimate=pl.CostEstimate(flops=flops, bytes_accessed=bytes_accessed, transcendentals=0),
        name=name,
    )(*ins)


def shape(dims, dtype):
    return jax.ShapeDtypeStruct(dims, dtype)


def halves(x):
    high = x.astype(BF16).astype(F32)
    return high, x - high


def pack_weights(pos, lengths, labels, partner, wq, wk, wv, score, out, ids, wvs, sems):
    copies = [
        pltpu.make_async_copy(wq, out.at[0:ROWS, 0:HEAD], sems.at[0]),
        pltpu.make_async_copy(wk, out.at[0:ROWS, HEAD : 2 * HEAD], sems.at[1]),
        pltpu.make_async_copy(wv, wvs, sems.at[2]),
    ]
    for copy in copies:
        copy.start()
    z, xl, c, window = pos[0], pos[1], pos[2], pos[3]
    here = xl * 2 + c
    for n, (dz, dx) in enumerate(ORDER):
        ids[n] = ((z + dz + NZ) % NZ) * 4 + (xl ^ dx) * 2 + c
    group = z * 4 + here
    mate = partner[group]
    ids[WINDOW] = window
    ids[GROUP] = group
    for k in range(NZ):
        ids[WANTED + k] = (partner[k * 4 + here] & 3) ^ here
    ids[MATE_STEP] = mate >> 2
    for n, x in enumerate((lengths[group], lengths[mate], labels[group], labels[mate], group, mate)):
        ids[HEADS + n] = x
    ids[CORE] = c
    for n, (dy, dx) in enumerate(AROUND):
        ids[OWN + n] = (((window >> 1) + dy) & 3) * 2 + ((window & 1) ^ dx)
    for copy in copies:
        copy.wait()
    s1, rest = halves(score[...])
    s2, s3 = halves(rest)
    row = lax.broadcasted_iota(jnp.int32, (EXT, HEAD), 0)
    lhs = jnp.where(row == 0, s1, jnp.where(row == 1, s2, jnp.where(row == 2, s3, 0.0)))
    product = lax.dot_general(lhs.astype(BF16), wvs[...], LAST, preferred_element_type=F32)
    total = jnp.sum(product, axis=0, keepdims=True)
    high, low = halves(total)
    row = lax.broadcasted_iota(jnp.int32, (EXT, ROWS), 0)
    ext = jnp.where((row == 0) | (row == 2), high, jnp.where(row == 1, low, 0.0))
    out[ROWS : ROWS + EXT, :] = ext.astype(BF16)
    for h in range(2):
        start = pl.multiple_of(window * SHARE + EXT * h, EXT)
        out[ROWS + EXT : BLOCK, HEAD * h : HEAD * (h + 1)] = wvs[pl.ds(start, EXT), :]


def split_columns(hidden, out):
    size, many = 4 * BLK, 4
    i = lax.broadcasted_iota(jnp.int32, (size, size), 0)
    o = lax.broadcasted_iota(jnp.int32, (size, size), 1)
    source = BLK * ((o & 127) >> 5) + SHARE * (o >> 7) + (o & 31)
    perm = jnp.where(i == source, 1.0, 0.0).astype(BF16)
    for h in range(2):
        for first in range(0, NDP // 4, many):
            x = [
                jnp.concatenate([hidden[:, ROWS * (4 * q + k) + BLK * h :][:, :BLK] for k in range(4)], axis=1)
                for q in range(first, first + many)
            ]
            y = jnp.dot(jnp.concatenate(x, axis=0), perm, preferred_element_type=F32).astype(BF16)
            for k in range(many):
                for r in range(4):
                    out[4 * h + r, :, BLK * (first + k) : BLK * (first + k + 1)] = y[BLK * k :][:BLK, BLK * r :][:, :BLK]


def project(first_block, count, ids, hidden, sibling, *refs):
    blocks, (out, kept, ahead, x, w, exts, sems, ahead_sems, out_sems) = refs[:count], refs[count:]

    def columns(n):
        return pl.ds(pl.multiple_of(ids[n] * ROWS, ROWS), ROWS)

    arrivals, leaving = [], []
    for n, block in enumerate(blocks):
        at = slice(ROWS * n, ROWS * (n + 1))
        pairs = (
            (block.at[0:ROWS], w.at[at]),
            (block.at[ROWS:BLOCK], exts.at[n]),
            (hidden.at[:, columns(first_block + n)], x.at[0:BLK, at]),
            (sibling.at[:, columns(first_block + n)], x.at[BLK : 2 * BLK, at]),
        )
        arrivals.append([pltpu.make_async_copy(a, b, sems.at[n, i]) for i, (a, b) in enumerate(pairs)])
        leaving.append(pltpu.make_async_copy(w.at[at], kept.at[n, 0:ROWS], out_sems.at[n, 0]))
        leaving.append(pltpu.make_async_copy(exts.at[n], kept.at[n, ROWS:BLOCK], out_sems.at[n, 1]))
    for group in arrivals:
        for copy in group:
            copy.start()
    handed = []
    for n in range(LAST_STEP):
        at = slice(ROWS * n, ROWS * (n + 1))
        for m, source in enumerate((hidden, sibling)):
            target = ahead.at[BLK * m : BLK * (m + 1), at]
            handed.append(
                pltpu.make_async_copy(source.at[:, columns(len(ORDER) - LAST_STEP + n)], target, ahead_sems.at[n, m])
            )
            handed[-1].start()
    acc = jnp.zeros((2 * BLK, 2 * HEAD), F32)
    wide = [jnp.zeros((BLK, BLK), F32)] * 2
    for first in range(0, count, 4):
        many = min(4, count - first)
        for n in range(first, first + many):
            for copy in arrivals[n]:
                copy.wait()
            leaving[2 * n].start()
            leaving[2 * n + 1].start()
        at = slice(ROWS * first, ROWS * (first + many))
        acc += jnp.dot(x[:, at], w[at, :], preferred_element_type=F32)
        for n in range(first, first + many):
            ext = exts[n, 0:EXT, :].astype(F32)
            row = ext[0:1] + ext[1:2]
            for m in range(2):
                product = x[BLK * m : BLK * (m + 1), ROWS * n : ROWS * (n + 1)].astype(F32) * row
                wide[m] += product[:, 0:BLK] + product[:, BLK : 2 * BLK]
    add_sums(None, acc, wide, out)
    for copy in handed + leaving:
        copy.wait()


def add_sums(sums, acc, wide, out):
    for m in range(2):
        qk = acc[BLK * m : BLK * (m + 1)]
        total = jnp.sum(wide[m].T, axis=0, keepdims=True)
        ext = jnp.broadcast_to(jnp.concatenate([total, total], axis=1), (8, 2 * HEAD))
        out[m, 0:BLK, :] = qk if sums is None else sums[m, 0:BLK, :] + qk
        out[m, BLK : BLK + 8, :] = ext if sums is None else sums[m, BLK : BLK + 8, :] + ext


def project_last(before, ahead, *refs):
    blocks, (out, kept, x, sums, sems) = refs[:LAST_STEP], refs[LAST_STEP:]
    pairs = [(block, kept.at[n]) for n, block in enumerate(blocks)] + [(ahead, x), (before, sums)]
    copies = [pltpu.make_async_copy(a, b, sems.at[n]) for n, (a, b) in enumerate(pairs)]
    for copy in copies:
        copy.start()
    for copy in copies:
        copy.wait()
    acc = jnp.zeros((2 * BLK, 2 * HEAD), F32)
    wide = [jnp.zeros((BLK, BLK), F32)] * 2
    for n in range(LAST_STEP):
        at = slice(ROWS * n, ROWS * (n + 1))
        acc += jnp.dot(x[:, at], kept[n, 0:ROWS, :], preferred_element_type=F32)
        ext = kept[n, ROWS : ROWS + EXT, :].astype(F32)
        row = ext[0:1] + ext[1:2]
        for m in range(2):
            product = x[BLK * m : BLK * (m + 1), at].astype(F32) * row
            wide[m] += product[:, 0:BLK] + product[:, BLK : 2 * BLK]
    add_sums(sums, acc, wide, out)


def join_cores(mine, theirs, items, first):
    row = lax.broadcasted_iota(jnp.int32, (EXT, 2 * HEAD), 0)
    for n in range(2):
        full = mine[n] + theirs[1 - n]
        high, low = halves(full[BLK : BLK + 1, 0:BLK])
        items[n, 0:BLK, :] = full[0:BLK].astype(BF16)
        items[n, BLK : BLK + EXT, :] = jnp.where(row == 0, jnp.concatenate([high, low], axis=1), 0.0).astype(BF16)
    first[...] = items[0]


def pick_for_planes(ids, near, side, out, items):
    items[0:2] = near[...]
    items[2:4] = side[...]
    for z in range(NZ):
        out[z] = items[ids[WANTED + z]]


def pick_partner(ids, received, out, mine, sem, sems):
    copy = pltpu.make_async_copy(received.at[ids[MATE_STEP]], mine, sem.at[0])
    copy.start()
    copy.wait()
    copies = [pltpu.make_async_copy(mine, out.at[s], sems.at[s]) for s in range(NSEQ)]
    for copy in copies:
        copy.start()
    for copy in copies:
        copy.wait()


def attention(
    ids,
    mate,
    own_0,
    own_1,
    own_2,
    own_3,
    own_4,
    own_5,
    own_6,
    own_7,
    hidden,
    kept_a,
    kept_b,
    swapped_a,
    swapped_b,
    keep,
    send,
    grads,
    crows,
    exts,
    k_t,
    q_own,
    k_own,
    q_mate,
    k_mate,
    wcol,
    scores,
    dots,
    dq,
    dk,
    cacc,
    all_grads,
    columns,
    value_parts,
    value_rows,
    shares,
    ext,
    sems,
    late_sems,
):
    pieces = [
        (mate.at[:, 0:BLK, 0:HEAD], q_mate),
        (mate.at[:, 0:BLK, HEAD : 2 * HEAD], k_mate),
        (mate.at[:, BLK : BLK + EXT, :], exts.at[0]),
    ]
    for n, ref in enumerate((own_0, own_1, own_2, own_3, own_4, own_5, own_6, own_7)):
        at = ids[OWN + n]
        pieces.append((ref.at[0:BLK, 0:HEAD], q_own.at[at]))
        pieces.append((ref.at[0:BLK, HEAD : 2 * HEAD], k_own.at[at]))
        pieces.append((ref.at[BLK : BLK + EXT, :], exts.at[1, at]))
    copies = [pltpu.make_async_copy(a, b, sems.at[n]) for n, (a, b) in enumerate(pieces)]
    for copy in copies:
        copy.start()
    late = [
        pltpu.make_async_copy(hidden, columns, late_sems.at[0]),
    ]
    for n, ref in enumerate((kept_a, kept_b, swapped_a, swapped_b)):
        first, count = PARTS[n % 2]
        part = value_parts.at[n // 2, first : first + count]
        late.append(pltpu.make_async_copy(ref.at[:, ROWS + EXT : BLOCK, :], part, late_sems.at[1 + n]))
    for copy in late:
        copy.start()
    cacc[...] = jnp.zeros_like(cacc)
    dk[...] = jnp.zeros_like(dk)
    for copy in copies:
        copy.wait()
    scale = 1.0 / math.sqrt(HEAD)
    exponent = scale * math.log2(math.e)
    own_len, mate_len = ids[HEADS], ids[HEADS + 1]
    for i in range(NSEQ):
        at = slice(BLK * i, BLK * (i + 1))
        k_t[:, at] = k_mate[i].astype(F32).T.astype(BF16)
        for n in range(2):
            extra = exts[n, i].astype(F32)
            row = extra[0:1, 0:BLK] + extra[0:1, BLK : 2 * BLK]
            wcol[n, at, :] = jnp.broadcast_to(row, (BLK, BLK)).T

    def softmax(side, queries, keys, start, key_len):
        q = queries[pl.ds(start // BLK, TB // BLK)].reshape(TB, HEAD)
        top = jnp.full((8, TB), -jnp.inf, F32)
        for u in range(NSEQ):
            at = slice(BLK * u, BLK * (u + 1))
            s = lax.dot_general(keys[u], q, LAST, preferred_element_type=F32)
            s = s * exponent + jnp.where(u < key_len, 0.0, -1e30).astype(F32)
            scores[side, at, :] = s
            top = jnp.maximum(top, jnp.max(s.reshape(BLK // 8, 8, TB), axis=0))
        top = jnp.max(top, axis=0, keepdims=True)
        total = jnp.zeros((8, TB), F32)
        weighed = jnp.zeros((8, TB), F32)
        for u in range(2 * NSEQ):
            at = slice(64 * u, 64 * (u + 1))
            e = jnp.exp2(scores[side, at, :] - top)
            scores[side, at, :] = e
            w = wcol[side, at, :]
            total += jnp.sum(e.reshape(8, 8, TB), axis=0)
            weighed += jnp.sum((e * jnp.concatenate([w, w], axis=1)).reshape(8, 8, TB), axis=0)
        total = jnp.sum(total, axis=0, keepdims=True)
        inverse = 1.0 / total
        s_row = jnp.sum(weighed, axis=0, keepdims=True) * inverse
        return inverse, s_row

    def live_row(start, length):
        t = lax.broadcasted_iota(jnp.int32, (1, TB), 1) + start
        return jnp.where(t < BLK * length, 1.0, 0.0).astype(F32)

    def first(n, z):
        side = 0
        start = pl.multiple_of(n * TB, TB)
        inverse, s_row = softmax(0, q_own, k_mate, start, mate_len)
        live = live_row(start, own_len)
        for u in range(2 * NSEQ):
            at = slice(64 * u, 64 * (u + 1))
            w = wcol[0, at, :]
            dots[side, at, :] = (scores[side, at, :] * (jnp.concatenate([w, w], axis=1) - s_row)).astype(BF16)
        g = jnp.dot(k_t[...], dots[side], preferred_element_type=F32)
        dq[:, pl.ds(start, TB)] = g * (inverse * live)
        return z + s_row * live

    def second(n, z):
        side = 1
        start = pl.multiple_of(n * TB, TB)
        inverse, s_row = softmax(1, q_mate, k_own, start, own_len)
        live = live_row(start, mate_len)
        r = inverse * live
        for u in range(2 * NSEQ):
            at = slice(64 * u, 64 * (u + 1))
            w = wcol[1, at, :]
            f = scores[side, at, :] * r
            cacc[at, :] += f[:, 0:BLK] + f[:, BLK:TB]
            dots[side, at, :] = (f * (jnp.concatenate([w, w], axis=1) - s_row)).astype(BF16)
        q = q_mate[pl.ds(start // BLK, TB // BLK)].reshape(TB, HEAD)
        dk[...] += jnp.dot(dots[side], q, preferred_element_type=F32)
        return z + s_row * live

    zero = jnp.zeros((1, TB), F32)

    def both(n, z):
        return first(n, z[0]), second(n, z[1])

    z_own, z_mate = lax.fori_loop(0, SEQLEN // TB, both, (zero, zero), unroll=SEQLEN // TB)

    def head(z_row, length, label, index):
        count = jnp.full((1, 1), BLK * length, jnp.int32).astype(F32)
        sign = jnp.full((1, 1), 2 * label - 1, jnp.int32).astype(F32)
        factor = 32.0 * (1.0 + 2.0 * jnp.full((1, 1), index, jnp.int32).astype(F32) / (NDP - 1))
        root = jnp.sqrt(count)
        x = -sign * (jnp.sum(z_row, axis=1, keepdims=True) / root)
        e = jnp.exp(-jnp.abs(x))
        term = factor * (jnp.maximum(x, 0.0) + jnp.log1p(e))
        sigmoid = jnp.where(x >= 0, 1.0, e) / (1.0 + e)
        return term, -factor * sign * sigmoid / root

    term, ds_own = head(z_own, own_len, ids[HEADS + 2], ids[HEADS + 4])
    _, ds_mate = head(z_mate, mate_len, ids[HEADS + 3], ids[HEADS + 5])
    row = lax.broadcasted_iota(jnp.int32, (EXT, BLK), 0)
    for i in range(NSEQ):
        at = slice(BLK * i, BLK * (i + 1))
        all_grads[0:HEAD, at] = (dq[:, at] * (ds_own * scale)).astype(BF16)
        all_grads[HEAD : 2 * HEAD, at] = (dk[at, :] * (ds_mate * scale)).T.astype(BF16)
        c_row = jnp.sum(cacc[at, :].T, axis=0, keepdims=True) * ds_mate
        high, low = halves(c_row)
        c_rows = jnp.where(row < 2, high, jnp.where(row == 2, low, 0.0)).astype(BF16)
        all_grads[2 * HEAD : 2 * HEAD + EXT, at] = c_rows

        @pl.when(ids[WINDOW] == i)
        def _(at=at, c_rows=c_rows):
            grads[...] = all_grads[0 : 2 * HEAD, at].astype(F32).T.astype(BF16)
            crows[...] = c_rows

    for copy in late:
        copy.wait()
    for flip in range(2):
        for n in range(len(ORDER)):
            for h in range(2):
                start = pl.multiple_of((ids[n] ^ flip) * SHARE + EXT * h, EXT)
                value_rows[pl.ds(start, EXT), :] = value_parts[flip, n, :, HEAD * h : HEAD * (h + 1)]
    chunk = 256
    wide = []
    for n in range(COLS // chunk):
        x = columns[:, :, chunk * n : chunk * (n + 1)].reshape(SEQLEN, chunk)
        y = jnp.dot(all_grads[...], x, preferred_element_type=F32)
        rows = y[0 : 2 * HEAD].T
        for k in range(chunk // SHARE):
            d = n * (chunk // SHARE) + k
            shares[(d & 1) ^ ids[CORE], d >> 1] = rows[SHARE * k : SHARE * (k + 1)]
        wide.append(y[2 * HEAD : 2 * HEAD + 1] + y[2 * HEAD + 2 : 2 * HEAD + 3])
    row = lax.broadcasted_iota(jnp.int32, (EXT, chunk), 0)
    gs = jnp.zeros((EXT, HEAD), F32)
    ext[...] = jnp.zeros_like(ext)
    for n, u in enumerate(wide):
        high, low = halves(u)
        ext[n : n + 1, :] = high
        ext[4 + n : 5 + n, :] = low
        lhs = jnp.where(row == 0, high, jnp.where(row == 1, low, 0.0)).astype(BF16)
        gs += jnp.dot(lhs, value_rows[chunk * n : chunk * (n + 1), :], preferred_element_type=F32)
    high, low = halves(gs[0:1] + gs[1:2])
    ext[8:9, 0:HEAD] = high
    ext[8:9, HEAD : 2 * HEAD] = low
    high, low = halves(jnp.broadcast_to(term, (1, HEAD)))
    ext[9:10, 0:HEAD] = high
    ext[9:10, HEAD : 2 * HEAD] = low
    tail = ext[...]
    for m in range(NDP // 2):
        keep[m, 0:SHARE, :] = shares[0, m]
        keep[m, SHARE : SHARE + EXT, :] = tail
        send[m, 0:SHARE, :] = shares[1, m].astype(BF16)
        send[m, SHARE : SHARE + EXT, :] = tail.astype(BF16)


def add_core(keep, received, out, ext):
    split_again(keep[0, SHARE : SHARE + EXT, :] + received[0, SHARE : SHARE + EXT, :].astype(F32), ext)
    tail = ext[...].astype(BF16)
    for m in range(NDP // 2):
        out[m, 0:SHARE, :] = (keep[m, 0:SHARE, :] + received[m, 0:SHARE, :].astype(F32)).astype(BF16)
        out[m, SHARE : SHARE + EXT, :] = tail


def split_again(tail, ext):
    ext[...] = jnp.zeros_like(ext)
    high, low = halves(tail[0:4] + tail[4:8])
    ext[0:4, :] = high
    ext[4:8, :] = low
    for n in (8, 9):
        high, low = halves(tail[n : n + 1, 0:HEAD] + tail[n : n + 1, HEAD : 2 * HEAD])
        ext[n : n + 1, 0:HEAD] = high
        ext[n : n + 1, HEAD : 2 * HEAD] = low


def sum_shares(received, out, ext):
    acc = received[0].astype(F32)
    for n in range(1, NDP // 2):
        acc += received[n].astype(F32)
    split_again(acc[SHARE : SHARE + EXT], ext)
    rows = acc[0:SHARE].astype(BF16)
    tail = ext[...].astype(BF16)
    for s in range(NSEQ):
        out[s, 0:SHARE, :] = rows
        out[s, SHARE : SHARE + EXT, :] = tail


def unpack(ids, received, score, gq, gk, gv, gs, loss):
    d = ids[GROUP]
    sub = lax.broadcasted_iota(jnp.int32, (4, 2 * HEAD), 0)
    lane = lax.broadcasted_iota(jnp.int32, (SHARE, 2 * HEAD), 1)
    j = lax.broadcasted_iota(jnp.int32, (SHARE, 2 * HEAD), 0)
    hit = lane == SHARE * (d % 8) + j
    readout = jnp.zeros((1, HEAD), F32)
    for s in range(NSEQ):
        at = slice(SHARE * s, SHARE * (s + 1))
        block = received[s].astype(F32)
        gq[at, :] = block[0:SHARE, 0:HEAD]
        gk[at, :] = block[0:SHARE, HEAD : 2 * HEAD]
        tail = block[SHARE : SHARE + EXT]
        u = tail[0:4] + tail[4:8]
        u = jnp.sum(jnp.where(sub == d // 8, u, 0.0), axis=0, keepdims=True)
        column = jnp.sum(jnp.where(hit, u, 0.0), axis=1, keepdims=True)
        gv[at, :] = column * score[...]
        readout += tail[8:9, 0:HEAD] + tail[8:9, HEAD : 2 * HEAD]
        if s == 0:
            loss[...] = tail[9:10, 0:HEAD] + tail[9:10, HEAD : 2 * HEAD]
    gs[...] = readout


def hidden_grads(ids, grads, crows, *refs):
    kept, out = refs[:-1], refs[-1]
    g = grads[...]
    c = crows[...].astype(F32).T.astype(BF16)
    for part, ref in enumerate(kept):
        first, count = PARTS[part % 2]
        for n in range(count):
            start = pl.multiple_of((ids[first + n] ^ (part // 2)) * ROWS, ROWS)
            y = lax.dot_general(g, ref[n, 0:ROWS, :], LAST, preferred_element_type=F32)
            y += jnp.dot(c, ref[n, ROWS : ROWS + EXT, :], preferred_element_type=F32)
            out[:, pl.ds(start, ROWS)] = y.astype(BF16)


SWAP = [(0, 1), (1, 0)]
UP = [(i, (i + 1) % NZ) for i in range(NZ)]
DOWN = [(i, (i - 1) % NZ) for i in range(NZ)]
ORDER = [(0, 0), (0, 1)]
for _step in range(1, NZ // 2 + 1):
    for _x in (0, 1):
        if _step < NZ // 2 or _x == 0:
            ORDER.append((-_step, _x))
        if _step < NZ // 2 or _x == 1:
            ORDER.append((_step, _x))


AROUND = [(0, 0), (0, 1), (1, 0), (1, 1), (-1, 0), (-1, 1), (2, 0), (2, 1)]
LAST_STEP = 4
PARTS = ((0, 12), (12, LAST_STEP))


def ring_step(found, key):
    dz, dx = key
    step, way = (1, UP) if dz < 0 else (-1, DOWN)
    found[key] = lax.ppermute(found[(dz + step, dx)], "z", way)


def per_device(hidden, w_query, w_key, w_value, score_vec, labels, lengths, partner):
    tokens = hidden.reshape(BLK, NDP * ROWS)
    score = score_vec.reshape(1, HEAD)
    z, xl, c = (lax.axis_index(a) for a in DP)
    window = lax.axis_index("y") * 2 + lax.axis_index("xh")
    pos = jnp.stack([z, xl, c, window]).astype(jnp.int32)
    item = (BLK + EXT, 2 * HEAD)

    block, ids = call(
        pack_weights,
        (shape((BLOCK, ROWS), BF16), shape((64,), jnp.int32)),
        (pos, lengths, labels, partner, w_query, w_key, w_value, score),
        far=(4, 5, 6),
        scratch=[pltpu.VMEM((ROWS, HEAD), BF16), pltpu.SemaphoreType.DMA((3,))],
        name="pack_weights",
        limit=62,
    )
    other = lax.ppermute(block, "xl", SWAP)
    sibling = lax.ppermute(tokens, "c", SWAP)
    up = lax.ppermute(block, "z", UP)
    down = lax.ppermute(block, "z", DOWN)
    later, _ = lax.optimization_barrier((tokens, block))
    split = call(split_columns, shape((NSEQ, BLK, COLS), BF16), (later,), name="split_columns", flops=1 << 30)
    found = {(0, 0): block, (0, 1): other, (-1, 0): up, (1, 0): down}
    second = ((-1, 1), (1, 1), (-2, 0), (2, 0))
    for key in second:
        ring_step(found, key)
    split, *arrived = lax.optimization_barrier((split, *[found[key] for key in second]))
    found.update(zip(second, arrived))
    hidden_t = lax.all_to_all(split, SEQ, 0, 0, tiled=True)
    for key in ORDER:
        if key not in found:
            ring_step(found, key)
    partial_shape = shape((2, BLK + 8, 2 * HEAD), F32)

    first, count = PARTS[0]
    partial, kept_early, ahead = call(
        functools.partial(project, first, count),
        (partial_shape, shape((count, BLOCK, ROWS), BF16), shape((2 * BLK, LAST_STEP * ROWS), BF16)),
        (ids, tokens, sibling, *[found[key] for key in ORDER[first : first + count]]),
        far=range(1, 3 + count),
        far_out=((count, BLOCK, ROWS),),
        scratch=[
            pltpu.VMEM((2 * BLK, count * ROWS), BF16),
            pltpu.VMEM((count * ROWS, ROWS), BF16),
            pltpu.VMEM((count, 2 * EXT, ROWS), BF16),
            pltpu.SemaphoreType.DMA((count, 4)),
            pltpu.SemaphoreType.DMA((LAST_STEP, 2)),
            pltpu.SemaphoreType.DMA((count, 2)),
        ],
        limit=62,
        name="project",
        flops=count << 25,
        bytes_accessed=count << 19,
    )
    partial, kept_late = call(
        project_last,
        (partial_shape, shape((LAST_STEP, BLOCK, ROWS), BF16)),
        (partial, ahead, *[found[key] for key in ORDER[-LAST_STEP:]]),
        far=range(2 + LAST_STEP),
        scratch=[
            pltpu.VMEM((2 * BLK, LAST_STEP * ROWS), BF16),
            pltpu.VMEM(partial_shape.shape, F32),
            pltpu.SemaphoreType.DMA((2 + LAST_STEP,)),
        ],
        limit=62,
        name="project_last",
        flops=LAST_STEP << 25,
    )
    theirs = lax.ppermute(partial, "c", SWAP)
    items, mine = call(
        join_cores, (shape((2, *item), BF16), shape(item, BF16)), (partial, theirs), name="join_cores"
    )
    side = lax.ppermute(items, "xl", SWAP)
    slots = call(
        pick_for_planes,
        shape((NZ, *item), BF16),
        (ids, items, side),
        scratch=[pltpu.VMEM((4, *item), BF16)],
        name="pick_for_planes",
    )
    slots, hidden_t, *kept = lax.optimization_barrier((slots, hidden_t, kept_early, kept_late))
    arrived = lax.all_to_all(slots, "z", 0, 0, tiled=True)
    kept += [lax.ppermute(part, "c", SWAP) for part in kept]
    windows = {(0, 0): mine, (0, 1): lax.ppermute(mine, "xh", SWAP)}
    for dy in (1, -1, 2):
        for dx in (0, 1):
            windows[(dy, dx)] = lax.ppermute(windows[(0, dx)], "y", [(i, (i - dy) % 4) for i in range(4)])
    arrived, *own = lax.optimization_barrier((arrived, *[windows[key] for key in AROUND]))
    theirs = call(
        pick_partner,
        shape((NSEQ, *item), BF16),
        (ids, arrived),
        far=(1,),
        far_out=((NSEQ, *item),),
        scratch=[pltpu.VMEM(item, BF16), pltpu.SemaphoreType.DMA((1,)), pltpu.SemaphoreType.DMA((NSEQ,))],
        name="pick_partner",
        limit=62,
    )
    mate = lax.all_to_all(theirs, SEQ, 0, 0, tiled=True)

    message = (NDP // 2, SHARE + EXT, 2 * HEAD)
    ext = pltpu.VMEM((EXT, 2 * HEAD), F32)
    keep, send, grads, crows = call(
        attention,
        (shape(message, F32), shape(message, BF16), shape((BLK, 2 * HEAD), BF16), shape((EXT, BLK), BF16)),
        (ids, mate, *own, hidden_t, *kept),
        far=range(1, 15),
        scratch=[
            pltpu.VMEM((2, NSEQ, EXT, 2 * HEAD), BF16),
            pltpu.VMEM((HEAD, SEQLEN), BF16),
            *[pltpu.VMEM((NSEQ, BLK, HEAD), BF16)] * 4,
            pltpu.VMEM((2, SEQLEN, BLK), F32),
            pltpu.VMEM((2, SEQLEN, TB), F32),
            pltpu.VMEM((2, SEQLEN, TB), BF16),
            pltpu.VMEM((HEAD, SEQLEN), F32),
            pltpu.VMEM((SEQLEN, HEAD), F32),
            pltpu.VMEM((SEQLEN, BLK), F32),
            pltpu.VMEM((2 * HEAD + EXT, SEQLEN), BF16),
            pltpu.VMEM((NSEQ, BLK, COLS), BF16),
            pltpu.VMEM((2, len(ORDER), EXT, ROWS), BF16),
            pltpu.VMEM((COLS, HEAD), BF16),
            pltpu.VMEM((2, NDP // 2, SHARE, 2 * HEAD), F32),
            ext,
            pltpu.SemaphoreType.DMA((27,)),
            pltpu.SemaphoreType.DMA((5,)),
        ],
        name="attention",
        limit=62,
        flops=1 << 31,
    )
    shares = call(add_core, shape(message, BF16), (keep, lax.ppermute(send, "c", SWAP)), scratch=[ext], name="add_core")
    arrived = lax.all_to_all(shares, ("z", "xl"), 0, 0, tiled=True)
    grad_hidden = call(
        hidden_grads,
        shape((BLK, NDP * ROWS), BF16),
        (ids, grads, crows, *kept),
        name="hidden_grads",
        flops=1 << 29,
        bytes_accessed=6 << 20,
    )
    arrived, grad_hidden = lax.optimization_barrier((arrived, grad_hidden))
    sums = call(
        sum_shares,
        shape((NSEQ, SHARE + EXT, 2 * HEAD), BF16),
        (arrived,),
        scratch=[ext],
        name="sum_shares",
    )
    arrived = lax.all_to_all(sums, SEQ, 0, 0, tiled=True)
    grad_query, grad_key, grad_value, grad_score, loss = call(
        unpack,
        (
            shape((ROWS, HEAD), F32),
            shape((ROWS, HEAD), F32),
            shape((ROWS, HEAD), F32),
            shape((1, HEAD), F32),
            shape((1, HEAD), F32),
        ),
        (ids, arrived, score),
        name="unpack",
    )
    return (
        loss[0, 0],
        grad_query,
        grad_key,
        grad_value,
        grad_score.reshape(HEAD),
        grad_hidden.reshape(1, BLK, NDP * ROWS),
    )


def solution(mesh):
    parts = Mesh(mesh.devices.reshape(NZ, NX, NC, 4, 2), DP + SEQ)
    return jax.shard_map(
        per_device,
        mesh=parts,
        in_specs=(P(DP, SEQ, None), P(DP, None), P(DP, None), P(DP, None), P(), P(), P(), P()),
        out_specs=(P(), P(DP, None), P(DP, None), P(DP, None), P(), P(DP, SEQ, None)),
        check_vma=False,
    )
```

```python
import functools
import math

import jax
import jax.numpy as jnp
from jax import lax
from jax.experimental import pallas as pl
from jax.experimental.pallas import tpu as pltpu
from jax.sharding import Mesh
from jax.sharding import PartitionSpec as P

F32 = jnp.float32
BF16 = jnp.bfloat16
NZ, NX, NC = 8, 2, 2
NDP = NZ * NX * NC
NSEQ = 8
BLK = 128
HEAD = 128
ROWS = 256
EXT = 16
BLOCK = ROWS + 2 * EXT
SHARE = ROWS // NSEQ
COLS = NDP * SHARE
MESSAGE = 2 * SHARE + EXT
SEQLEN = NSEQ * BLK
TB = 256
DP = ("z", "xl", "c")
SEQ = ("y", "xh")
LAST = (((1,), (1,)), ((), ()))
VM = pl.BlockSpec(memory_space=pltpu.VMEM)
SM = pl.BlockSpec(memory_space=pltpu.SMEM)
HBM = pl.BlockSpec(memory_space=pltpu.HBM)
WINDOW, GROUP, WANTED, MATE_STEP, HEADS, CORE, OWN = 16, 17, 18, 26, 27, 33, 34


def call(kernel, outs, ins, scratch=(), far=(), far_out=(), flops=0, bytes_accessed=0, name=None, limit=48):
    return pl.pallas_call(
        kernel,
        out_shape=outs,
        in_specs=[SM if a.dtype == jnp.int32 else HBM if n in far else VM for n, a in enumerate(ins)],
        out_specs=jax.tree.map(lambda o: SM if o.dtype == jnp.int32 else HBM if o.shape in far_out else VM, outs),
        scratch_shapes=list(scratch),
        compiler_params=pltpu.CompilerParams(vmem_limit_bytes=limit * 1024 * 1024),
        cost_estimate=pl.CostEstimate(flops=flops, bytes_accessed=bytes_accessed, transcendentals=0),
        name=name,
    )(*ins)


def shape(dims, dtype):
    return jax.ShapeDtypeStruct(dims, dtype)


def halves(x):
    high = x.astype(BF16).astype(F32)
    return high, x - high


def pack_weights(pos, lengths, labels, partner, wq, wk, wv, score, out, ids, wvs, sems):
    copies = [
        pltpu.make_async_copy(wq, out.at[0:ROWS, 0:HEAD], sems.at[0]),
        pltpu.make_async_copy(wk, out.at[0:ROWS, HEAD : 2 * HEAD], sems.at[1]),
        pltpu.make_async_copy(wv, wvs, sems.at[2]),
    ]
    for copy in copies:
        copy.start()
    z, xl, c, window = pos[0], pos[1], pos[2], pos[3]
    here = xl * 2 + c
    for n, (dz, dx) in enumerate(ORDER):
        ids[n] = ((z + dz + NZ) % NZ) * 4 + (xl ^ dx) * 2 + c
    group = z * 4 + here
    mate = partner[group]
    ids[WINDOW] = window
    ids[GROUP] = group
    for k in range(NZ):
        ids[WANTED + k] = (partner[k * 4 + here] & 3) ^ here
    ids[MATE_STEP] = mate >> 2
    for n, x in enumerate((lengths[group], lengths[mate], labels[group], labels[mate], group, mate)):
        ids[HEADS + n] = x
    ids[CORE] = c
    for n, (dy, dx) in enumerate(AROUND):
        ids[OWN + n] = (((window >> 1) + dy) & 3) * 2 + ((window & 1) ^ dx)
    for copy in copies:
        copy.wait()
    s1, rest = halves(score[...])
    s2, s3 = halves(rest)
    row = lax.broadcasted_iota(jnp.int32, (EXT, HEAD), 0)
    lhs = jnp.where(row == 0, s1, jnp.where(row == 1, s2, jnp.where(row == 2, s3, 0.0)))
    product = lax.dot_general(lhs.astype(BF16), wvs[...], LAST, preferred_element_type=F32)
    total = jnp.sum(product, axis=0, keepdims=True)
    high, low = halves(total)
    row = lax.broadcasted_iota(jnp.int32, (EXT, ROWS), 0)
    ext = jnp.where((row == 0) | (row == 2), high, jnp.where(row == 1, low, 0.0))
    out[ROWS : ROWS + EXT, :] = ext.astype(BF16)
    for h in range(2):
        start = pl.multiple_of(window * SHARE + EXT * h, EXT)
        out[ROWS + EXT : BLOCK, HEAD * h : HEAD * (h + 1)] = wvs[pl.ds(start, EXT), :]


def split_columns(hidden, out):
    size, many = 4 * BLK, 4
    i = lax.broadcasted_iota(jnp.int32, (size, size), 0)
    o = lax.broadcasted_iota(jnp.int32, (size, size), 1)
    source = BLK * ((o & 127) >> 5) + SHARE * (o >> 7) + (o & 31)
    perm = jnp.where(i == source, 1.0, 0.0).astype(BF16)
    for h in range(2):
        for first in range(0, NDP // 4, many):
            x = [
                jnp.concatenate([hidden[:, ROWS * (4 * q + k) + BLK * h :][:, :BLK] for k in range(4)], axis=1)
                for q in range(first, first + many)
            ]
            y = jnp.dot(jnp.concatenate(x, axis=0), perm, preferred_element_type=F32).astype(BF16)
            for k in range(many):
                for r in range(4):
                    out[4 * h + r, :, BLK * (first + k) : BLK * (first + k + 1)] = y[BLK * k :][:BLK, BLK * r :][:, :BLK]


def project(ids, hidden, sibling, *refs):
    count = len(ORDER)
    blocks, (out, x, w, exts, sems) = refs[:count], refs[count:]
    arrivals = []
    for n, block in enumerate(blocks):
        columns = pl.ds(pl.multiple_of(ids[n] * ROWS, ROWS), ROWS)
        at = slice(ROWS * n, ROWS * (n + 1))
        pairs = (
            (block.at[0:ROWS], w.at[at]),
            (block.at[ROWS : ROWS + EXT], exts.at[n]),
            (hidden.at[:, columns], x.at[0:BLK, at]),
            (sibling.at[:, columns], x.at[BLK : 2 * BLK, at]),
        )
        arrivals.append([pltpu.make_async_copy(a, b, sems.at[n, i]) for i, (a, b) in enumerate(pairs)])
        for copy in arrivals[n]:
            copy.start()
    acc = jnp.zeros((2 * BLK, 2 * HEAD), F32)
    wide = [jnp.zeros((BLK, BLK), F32)] * 2
    many = 4
    for first in range(0, count, many):
        for group in arrivals[first : first + many]:
            for copy in group:
                copy.wait()
        at = slice(ROWS * first, ROWS * (first + many))
        acc += jnp.dot(x[:, at], w[at, :], preferred_element_type=F32)
        for n in range(first, first + many):
            ext = exts[n].astype(F32)
            row = ext[0:1] + ext[1:2]
            for m in range(2):
                product = x[BLK * m : BLK * (m + 1), ROWS * n : ROWS * (n + 1)].astype(F32) * row
                wide[m] += product[:, 0:BLK] + product[:, BLK : 2 * BLK]
    for m in range(2):
        total = jnp.sum(wide[m].T, axis=0, keepdims=True)
        out[m, 0:BLK, :] = acc[BLK * m : BLK * (m + 1)]
        out[m, BLK : BLK + 8, :] = jnp.broadcast_to(jnp.concatenate([total, total], axis=1), (8, 2 * HEAD))


def stack_blocks(*refs):
    blocks, (out, held, sems, out_sem) = refs[: len(ORDER)], refs[len(ORDER) :]
    copies = [pltpu.make_async_copy(block, held.at[n], sems.at[n]) for n, block in enumerate(blocks)]
    for copy in copies:
        copy.start()
    for copy in copies:
        copy.wait()
    copy = pltpu.make_async_copy(held, out, out_sem.at[0])
    copy.start()
    copy.wait()


def join_cores(mine, theirs, items, first):
    row = lax.broadcasted_iota(jnp.int32, (EXT, 2 * HEAD), 0)
    for n in range(2):
        full = mine[n] + theirs[1 - n]
        high, low = halves(full[BLK : BLK + 1, 0:BLK])
        items[n, 0:BLK, :] = full[0:BLK].astype(BF16)
        items[n, BLK : BLK + EXT, :] = jnp.where(row == 0, jnp.concatenate([high, low], axis=1), 0.0).astype(BF16)
    first[...] = items[0]


def pick_for_planes(ids, near, side, out, items):
    items[0:2] = near[...]
    items[2:4] = side[...]
    for z in range(NZ):
        out[z] = items[ids[WANTED + z]]


def pick_partner(ids, received, out, mine, sem, sems):
    copy = pltpu.make_async_copy(received.at[ids[MATE_STEP]], mine, sem.at[0])
    copy.start()
    copy.wait()
    copies = [pltpu.make_async_copy(mine, out.at[s], sems.at[s]) for s in range(NSEQ)]
    for copy in copies:
        copy.start()
    for copy in copies:
        copy.wait()


def attention(
    ids,
    mate,
    own_0,
    own_1,
    own_2,
    own_3,
    own_4,
    own_5,
    own_6,
    own_7,
    hidden,
    kept,
    swapped,
    keep,
    send,
    grads,
    crows,
    exts,
    k_t,
    q_own,
    k_own,
    q_mate,
    k_mate,
    wcol,
    scores,
    dots,
    dq,
    dk,
    cacc,
    all_grads,
    columns,
    value_parts,
    value_rows,
    shares,
    ext,
    sems,
    late_sems,
):
    pieces = [
        (mate.at[:, 0:BLK, 0:HEAD], q_mate),
        (mate.at[:, 0:BLK, HEAD : 2 * HEAD], k_mate),
        (mate.at[:, BLK : BLK + EXT, :], exts.at[0]),
    ]
    for n, ref in enumerate((own_0, own_1, own_2, own_3, own_4, own_5, own_6, own_7)):
        at = ids[OWN + n]
        pieces.append((ref.at[0:BLK, 0:HEAD], q_own.at[at]))
        pieces.append((ref.at[0:BLK, HEAD : 2 * HEAD], k_own.at[at]))
        pieces.append((ref.at[BLK : BLK + EXT, :], exts.at[1, at]))
    copies = [pltpu.make_async_copy(a, b, sems.at[n]) for n, (a, b) in enumerate(pieces)]
    for copy in copies:
        copy.start()
    late = [
        pltpu.make_async_copy(hidden, columns, late_sems.at[0]),
    ]
    for n, ref in enumerate((kept, swapped)):
        late.append(pltpu.make_async_copy(ref.at[:, ROWS + EXT : BLOCK, :], value_parts.at[n], late_sems.at[1 + n]))
    for copy in late:
        copy.start()
    cacc[...] = jnp.zeros_like(cacc)
    dk[...] = jnp.zeros_like(dk)
    for copy in copies:
        copy.wait()
    scale = 1.0 / math.sqrt(HEAD)
    exponent = scale * math.log2(math.e)
    own_len, mate_len = ids[HEADS], ids[HEADS + 1]
    for i in range(NSEQ):
        at = slice(BLK * i, BLK * (i + 1))
        k_t[:, at] = k_mate[i].astype(F32).T.astype(BF16)
        for n in range(2):
            extra = exts[n, i].astype(F32)
            row = extra[0:1, 0:BLK] + extra[0:1, BLK : 2 * BLK]
            wcol[n, at, :] = jnp.broadcast_to(row, (BLK, BLK)).T

    def softmax(side, queries, keys, start, key_len):
        q = queries[pl.ds(start // BLK, TB // BLK)].reshape(TB, HEAD)
        top = jnp.full((8, TB), -jnp.inf, F32)
        for u in range(NSEQ):
            at = slice(BLK * u, BLK * (u + 1))
            s = lax.dot_general(keys[u], q, LAST, preferred_element_type=F32)
            s = s * exponent + jnp.where(u < key_len, 0.0, -1e30).astype(F32)
            scores[side, at, :] = s
            top = jnp.maximum(top, jnp.max(s.reshape(BLK // 8, 8, TB), axis=0))
        top = jnp.max(top, axis=0, keepdims=True)
        total = jnp.zeros((8, TB), F32)
        weighed = jnp.zeros((8, TB), F32)
        for u in range(2 * NSEQ):
            at = slice(64 * u, 64 * (u + 1))
            e = jnp.exp2(scores[side, at, :] - top)
            scores[side, at, :] = e
            w = wcol[side, at, :]
            total += jnp.sum(e.reshape(8, 8, TB), axis=0)
            weighed += jnp.sum((e * jnp.concatenate([w, w], axis=1)).reshape(8, 8, TB), axis=0)
        total = jnp.sum(total, axis=0, keepdims=True)
        inverse = 1.0 / total
        s_row = jnp.sum(weighed, axis=0, keepdims=True) * inverse
        return inverse, s_row

    def live_row(start, length):
        t = lax.broadcasted_iota(jnp.int32, (1, TB), 1) + start
        return jnp.where(t < BLK * length, 1.0, 0.0).astype(F32)

    def first(n, z):
        side = 0
        start = pl.multiple_of(n * TB, TB)
        inverse, s_row = softmax(0, q_own, k_mate, start, mate_len)
        live = live_row(start, own_len)
        for u in range(2 * NSEQ):
            at = slice(64 * u, 64 * (u + 1))
            w = wcol[0, at, :]
            dots[side, at, :] = (scores[side, at, :] * (jnp.concatenate([w, w], axis=1) - s_row)).astype(BF16)
        g = jnp.dot(k_t[...], dots[side], preferred_element_type=F32)
        dq[:, pl.ds(start, TB)] = g * (inverse * live)
        return z + s_row * live

    def second(n, z):
        side = 1
        start = pl.multiple_of(n * TB, TB)
        inverse, s_row = softmax(1, q_mate, k_own, start, own_len)
        live = live_row(start, mate_len)
        r = inverse * live
        for u in range(2 * NSEQ):
            at = slice(64 * u, 64 * (u + 1))
            w = wcol[1, at, :]
            f = scores[side, at, :] * r
            cacc[at, :] += f[:, 0:BLK] + f[:, BLK:TB]
            dots[side, at, :] = (f * (jnp.concatenate([w, w], axis=1) - s_row)).astype(BF16)
        q = q_mate[pl.ds(start // BLK, TB // BLK)].reshape(TB, HEAD)
        dk[...] += jnp.dot(dots[side], q, preferred_element_type=F32)
        return z + s_row * live

    zero = jnp.zeros((1, TB), F32)

    def both(n, z):
        return first(n, z[0]), second(n, z[1])

    z_own, z_mate = lax.fori_loop(0, SEQLEN // TB, both, (zero, zero), unroll=SEQLEN // TB)

    def head(z_row, length, label, index):
        count = jnp.full((1, 1), BLK * length, jnp.int32).astype(F32)
        sign = jnp.full((1, 1), 2 * label - 1, jnp.int32).astype(F32)
        factor = 32.0 * (1.0 + 2.0 * jnp.full((1, 1), index, jnp.int32).astype(F32) / (NDP - 1))
        root = jnp.sqrt(count)
        x = -sign * (jnp.sum(z_row, axis=1, keepdims=True) / root)
        e = jnp.exp(-jnp.abs(x))
        term = factor * (jnp.maximum(x, 0.0) + jnp.log1p(e))
        sigmoid = jnp.where(x >= 0, 1.0, e) / (1.0 + e)
        return term, -factor * sign * sigmoid / root

    term, ds_own = head(z_own, own_len, ids[HEADS + 2], ids[HEADS + 4])
    _, ds_mate = head(z_mate, mate_len, ids[HEADS + 3], ids[HEADS + 5])
    row = lax.broadcasted_iota(jnp.int32, (EXT, BLK), 0)
    for i in range(NSEQ):
        at = slice(BLK * i, BLK * (i + 1))
        all_grads[0:HEAD, at] = (dq[:, at] * (ds_own * scale)).astype(BF16)
        all_grads[HEAD : 2 * HEAD, at] = (dk[at, :] * (ds_mate * scale)).T.astype(BF16)
        c_row = jnp.sum(cacc[at, :].T, axis=0, keepdims=True) * ds_mate
        high, low = halves(c_row)
        c_rows = jnp.where(row < 2, high, jnp.where(row == 2, low, 0.0)).astype(BF16)
        all_grads[2 * HEAD : 2 * HEAD + EXT, at] = c_rows

        @pl.when(ids[WINDOW] == i)
        def _(at=at, c_rows=c_rows):
            grads[...] = all_grads[0 : 2 * HEAD, at].astype(F32).T.astype(BF16)
            crows[...] = c_rows

    for copy in late:
        copy.wait()
    for flip in range(2):
        for n in range(len(ORDER)):
            for h in range(2):
                start = pl.multiple_of((ids[n] ^ flip) * SHARE + EXT * h, EXT)
                value_rows[pl.ds(start, EXT), :] = value_parts[flip, n, :, HEAD * h : HEAD * (h + 1)]
    chunk = 256
    wide = []
    for n in range(COLS // chunk):
        x = columns[:, :, chunk * n : chunk * (n + 1)].reshape(SEQLEN, chunk)
        y = jnp.dot(all_grads[...], x, preferred_element_type=F32)
        rows = y[0 : 2 * HEAD].T
        for k in range(chunk // SHARE):
            d = n * (chunk // SHARE) + k
            for h in range(2):
                part = rows[SHARE * k : SHARE * (k + 1), HEAD * h : HEAD * (h + 1)]
                shares[(d & 1) ^ ids[CORE], d >> 1, SHARE * h : SHARE * (h + 1), :] = part
        wide.append(y[2 * HEAD : 2 * HEAD + 1] + y[2 * HEAD + 2 : 2 * HEAD + 3])
    row = lax.broadcasted_iota(jnp.int32, (EXT, chunk), 0)
    gs = jnp.zeros((EXT, HEAD), F32)
    ext[...] = jnp.zeros_like(ext)
    for n, u in enumerate(wide):
        high, low = halves(u)
        ext[2 * n : 2 * n + 1, :] = u[:, 0:HEAD]
        ext[2 * n + 1 : 2 * n + 2, :] = u[:, HEAD : 2 * HEAD]
        lhs = jnp.where(row == 0, high, jnp.where(row == 1, low, 0.0)).astype(BF16)
        gs += jnp.dot(lhs, value_rows[chunk * n : chunk * (n + 1), :], preferred_element_type=F32)
    for n, total in ((8, gs[0:1] + gs[1:2]), (10, jnp.broadcast_to(term, (1, HEAD)))):
        high, low = halves(total)
        ext[n : n + 1, :] = high
        ext[n + 1 : n + 2, :] = low
    tail = ext[...]
    for m in range(NDP // 2):
        keep[m, 0 : 2 * SHARE, :] = shares[0, m]
        keep[m, 2 * SHARE : MESSAGE, :] = tail
        send[m, 0 : 2 * SHARE, :] = shares[1, m].astype(BF16)
        send[m, 2 * SHARE : MESSAGE, :] = tail.astype(BF16)


def add_core(keep, received, out, ext):
    split_again(keep[0, 2 * SHARE : MESSAGE, :] + received[0, 2 * SHARE : MESSAGE, :].astype(F32), ext)
    tail = ext[...].astype(BF16)
    for m in range(NDP // 2):
        out[m, 0 : 2 * SHARE, :] = (keep[m, 0 : 2 * SHARE, :] + received[m, 0 : 2 * SHARE, :].astype(F32)).astype(BF16)
        out[m, 2 * SHARE : MESSAGE, :] = tail


def split_again(tail, ext):
    ext[...] = tail
    for n in (8, 10):
        high, low = halves(tail[n : n + 1] + tail[n + 1 : n + 2])
        ext[n : n + 1, :] = high
        ext[n + 1 : n + 2, :] = low


def sum_shares(received, out, ext):
    acc = received[0].astype(F32)
    for n in range(1, NDP // 2):
        acc += received[n].astype(F32)
    split_again(acc[2 * SHARE : MESSAGE], ext)
    rows = acc[0 : 2 * SHARE].astype(BF16)
    tail = ext[...].astype(BF16)
    for s in range(NSEQ):
        out[s, 0 : 2 * SHARE, :] = rows
        out[s, 2 * SHARE : MESSAGE, :] = tail


def unpack(ids, received, score, gq, gk, gv, gs, loss):
    d = ids[GROUP]
    sub = lax.broadcasted_iota(jnp.int32, (8, HEAD), 0)
    lane = lax.broadcasted_iota(jnp.int32, (SHARE, HEAD), 1)
    j = lax.broadcasted_iota(jnp.int32, (SHARE, HEAD), 0)
    hit = lane == SHARE * (d & 3) + j
    readout = jnp.zeros((1, HEAD), F32)
    for s in range(NSEQ):
        at = slice(SHARE * s, SHARE * (s + 1))
        block = received[s].astype(F32)
        gq[at, :] = block[0:SHARE]
        gk[at, :] = block[SHARE : 2 * SHARE]
        tail = block[2 * SHARE : MESSAGE]
        u = jnp.sum(jnp.where(sub == d >> 2, tail[0:8], 0.0), axis=0, keepdims=True)
        column = jnp.sum(jnp.where(hit, u, 0.0), axis=1, keepdims=True)
        gv[at, :] = column * score[...]
        readout += tail[8:9] + tail[9:10]
        if s == 0:
            loss[...] = tail[10:11] + tail[11:12]
    gs[...] = readout


def hidden_grads(ids, grads, crows, kept, swapped, out):
    g = grads[...]
    c = crows[...].astype(F32).T.astype(BF16)
    for flip, ref in enumerate((kept, swapped)):
        for n in range(len(ORDER)):
            start = pl.multiple_of((ids[n] ^ flip) * ROWS, ROWS)
            y = lax.dot_general(g, ref[n, 0:ROWS, :], LAST, preferred_element_type=F32)
            y += jnp.dot(c, ref[n, ROWS : ROWS + EXT, :], preferred_element_type=F32)
            out[:, pl.ds(start, ROWS)] = y.astype(BF16)


SWAP = [(0, 1), (1, 0)]
UP = [(i, (i + 1) % NZ) for i in range(NZ)]
DOWN = [(i, (i - 1) % NZ) for i in range(NZ)]
ORDER = [(0, 0), (0, 1)]
for _step in range(1, NZ // 2 + 1):
    for _x in (0, 1):
        if _step < NZ // 2 or _x == 0:
            ORDER.append((-_step, _x))
        if _step < NZ // 2 or _x == 1:
            ORDER.append((_step, _x))


AROUND = [(0, 0), (0, 1), (1, 0), (1, 1), (-1, 0), (-1, 1), (2, 0), (2, 1)]
def ring_step(found, key):
    dz, dx = key
    step, way = (1, UP) if dz < 0 else (-1, DOWN)
    found[key] = lax.ppermute(found[(dz + step, dx)], "z", way)


def per_device(hidden, w_query, w_key, w_value, score_vec, labels, lengths, partner):
    tokens = hidden.reshape(BLK, NDP * ROWS)
    score = score_vec.reshape(1, HEAD)
    z, xl, c = (lax.axis_index(a) for a in DP)
    window = lax.axis_index("y") * 2 + lax.axis_index("xh")
    pos = jnp.stack([z, xl, c, window]).astype(jnp.int32)
    item = (BLK + EXT, 2 * HEAD)

    block, ids = call(
        pack_weights,
        (shape((BLOCK, ROWS), BF16), shape((64,), jnp.int32)),
        (pos, lengths, labels, partner, w_query, w_key, w_value, score),
        far=(4, 5, 6),
        scratch=[pltpu.VMEM((ROWS, HEAD), BF16), pltpu.SemaphoreType.DMA((3,))],
        name="pack_weights",
        limit=62,
    )
    other = lax.ppermute(block, "xl", SWAP)
    sibling = lax.ppermute(tokens, "c", SWAP)
    up = lax.ppermute(block, "z", UP)
    down = lax.ppermute(block, "z", DOWN)
    later, _ = lax.optimization_barrier((tokens, block))
    split = call(split_columns, shape((NSEQ, BLK, COLS), BF16), (later,), name="split_columns", flops=1 << 30)
    split, other, up, down = lax.optimization_barrier((split, other, up, down))
    found = {(0, 0): block, (0, 1): other, (-1, 0): up, (1, 0): down}
    hidden_t = lax.all_to_all(split, SEQ, 0, 0, tiled=True)
    for key in ORDER:
        if key not in found:
            ring_step(found, key)
    count = len(ORDER)
    blocks = [found[key] for key in ORDER]
    partial = call(
        project,
        shape((2, BLK + 8, 2 * HEAD), F32),
        (ids, tokens, sibling, *blocks),
        far=range(1, 3 + count),
        scratch=[
            pltpu.VMEM((2 * BLK, count * ROWS), BF16),
            pltpu.VMEM((count * ROWS, ROWS), BF16),
            pltpu.VMEM((count, EXT, ROWS), BF16),
            pltpu.SemaphoreType.DMA((count, 4)),
        ],
        limit=62,
        name="project",
        flops=1 << 29,
        bytes_accessed=6 << 20,
    )
    theirs = lax.ppermute(partial, "c", SWAP)
    items, mine = call(
        join_cores, (shape((2, *item), BF16), shape(item, BF16)), (partial, theirs), name="join_cores"
    )
    side = lax.ppermute(items, "xl", SWAP)
    slots = call(
        pick_for_planes,
        shape((NZ, *item), BF16),
        (ids, items, side),
        scratch=[pltpu.VMEM((4, *item), BF16)],
        name="pick_for_planes",
    )
    slots, hidden_t, *blocks = lax.optimization_barrier((slots, hidden_t, *blocks))
    arrived = lax.all_to_all(slots, "z", 0, 0, tiled=True)
    kept = call(
        stack_blocks,
        shape((count, BLOCK, ROWS), BF16),
        blocks,
        far=range(count),
        far_out=((count, BLOCK, ROWS),),
        scratch=[
            pltpu.VMEM((count, BLOCK, ROWS), BF16),
            pltpu.SemaphoreType.DMA((count,)),
            pltpu.SemaphoreType.DMA((1,)),
        ],
        limit=62,
        name="stack_blocks",
        bytes_accessed=5 << 20,
    )
    windows = {(0, 0): mine, (0, 1): lax.ppermute(mine, "xh", SWAP)}
    for dy in (1, -1, 2):
        for dx in (0, 1):
            windows[(dy, dx)] = lax.ppermute(windows[(0, dx)], "y", [(i, (i - dy) % 4) for i in range(4)])
    arrived, kept, *own = lax.optimization_barrier((arrived, kept, *[windows[key] for key in AROUND]))
    swapped = lax.ppermute(kept, "c", SWAP)
    theirs = call(
        pick_partner,
        shape((NSEQ, *item), BF16),
        (ids, arrived),
        far=(1,),
        far_out=((NSEQ, *item),),
        scratch=[pltpu.VMEM(item, BF16), pltpu.SemaphoreType.DMA((1,)), pltpu.SemaphoreType.DMA((NSEQ,))],
        name="pick_partner",
        limit=62,
    )
    mate = lax.all_to_all(theirs, SEQ, 0, 0, tiled=True)

    message = (NDP // 2, MESSAGE, HEAD)
    ext = pltpu.VMEM((EXT, HEAD), F32)
    keep, send, grads, crows = call(
        attention,
        (shape(message, F32), shape(message, BF16), shape((BLK, 2 * HEAD), BF16), shape((EXT, BLK), BF16)),
        (ids, mate, *own, hidden_t, kept, swapped),
        far=range(1, 13),
        scratch=[
            pltpu.VMEM((2, NSEQ, EXT, 2 * HEAD), BF16),
            pltpu.VMEM((HEAD, SEQLEN), BF16),
            *[pltpu.VMEM((NSEQ, BLK, HEAD), BF16)] * 4,
            pltpu.VMEM((2, SEQLEN, BLK), F32),
            pltpu.VMEM((2, SEQLEN, TB), F32),
            pltpu.VMEM((2, SEQLEN, TB), BF16),
            pltpu.VMEM((HEAD, SEQLEN), F32),
            pltpu.VMEM((SEQLEN, HEAD), F32),
            pltpu.VMEM((SEQLEN, BLK), F32),
            pltpu.VMEM((2 * HEAD + EXT, SEQLEN), BF16),
            pltpu.VMEM((NSEQ, BLK, COLS), BF16),
            pltpu.VMEM((2, len(ORDER), EXT, ROWS), BF16),
            pltpu.VMEM((COLS, HEAD), BF16),
            pltpu.VMEM((2, NDP // 2, 2 * SHARE, HEAD), F32),
            ext,
            pltpu.SemaphoreType.DMA((27,)),
            pltpu.SemaphoreType.DMA((3,)),
        ],
        name="attention",
        limit=62,
        flops=1 << 31,
    )
    shares = call(add_core, shape(message, BF16), (keep, lax.ppermute(send, "c", SWAP)), scratch=[ext], name="add_core")
    arrived = lax.all_to_all(shares, ("z", "xl"), 0, 0, tiled=True)
    grad_hidden = call(
        hidden_grads,
        shape((BLK, NDP * ROWS), BF16),
        (ids, grads, crows, kept, swapped),
        name="hidden_grads",
        flops=1 << 29,
        bytes_accessed=6 << 20,
    )
    arrived, grad_hidden = lax.optimization_barrier((arrived, grad_hidden))
    sums = call(
        sum_shares,
        shape((NSEQ, MESSAGE, HEAD), BF16),
        (arrived,),
        scratch=[ext],
        name="sum_shares",
    )
    arrived = lax.all_to_all(sums, SEQ, 0, 0, tiled=True)
    grad_query, grad_key, grad_value, grad_score, loss = call(
        unpack,
        (
            shape((ROWS, HEAD), F32),
            shape((ROWS, HEAD), F32),
            shape((ROWS, HEAD), F32),
            shape((1, HEAD), F32),
            shape((1, HEAD), F32),
        ),
        (ids, arrived, score),
        name="unpack",
    )
    return (
        loss[0, 0],
        grad_query,
        grad_key,
        grad_value,
        grad_score.reshape(HEAD),
        grad_hidden.reshape(1, BLK, NDP * ROWS),
    )


def solution(mesh):
    parts = Mesh(mesh.devices.reshape(NZ, NX, NC, 4, 2), DP + SEQ)
    return jax.shard_map(
        per_device,
        mesh=parts,
        in_specs=(P(DP, SEQ, None), P(DP, None), P(DP, None), P(DP, None), P(), P(), P(), P()),
        out_specs=(P(), P(DP, None), P(DP, None), P(DP, None), P(), P(DP, SEQ, None)),
        check_vma=False,
    )
```

```python
import math

import jax
import jax.numpy as jnp
from jax import lax
from jax.experimental import pallas as pl
from jax.experimental.pallas import tpu as pltpu
from jax.sharding import Mesh
from jax.sharding import PartitionSpec as P

F32 = jnp.float32
BF16 = jnp.bfloat16
NZ, NX, NC = 8, 2, 2
NDP = NZ * NX * NC
NSEQ = 8
BLK = 128
HEAD = 128
ROWS = 256
EXT = 16
BLOCK = ROWS + 2 * EXT
SHARE = ROWS // NSEQ
COLS = NDP * SHARE
MESSAGE = 2 * SHARE + EXT
SEQLEN = NSEQ * BLK
TB = 256
DP = ("z", "xl", "c")
SEQ = ("y", "xh")
LAST = (((1,), (1,)), ((), ()))
VM = pl.BlockSpec(memory_space=pltpu.VMEM)
SM = pl.BlockSpec(memory_space=pltpu.SMEM)
HBM = pl.BlockSpec(memory_space=pltpu.HBM)
WINDOW, GROUP, WANTED, MATE_STEP, HEADS, CORE, OWN = 16, 17, 18, 26, 27, 33, 34


def call(kernel, outs, ins, scratch=(), far=(), far_out=(), flops=0, bytes_accessed=0, name=None, limit=48):
    return pl.pallas_call(
        kernel,
        out_shape=outs,
        in_specs=[SM if a.dtype == jnp.int32 else HBM if n in far else VM for n, a in enumerate(ins)],
        out_specs=jax.tree.map(lambda o: SM if o.dtype == jnp.int32 else HBM if o.shape in far_out else VM, outs),
        scratch_shapes=list(scratch),
        compiler_params=pltpu.CompilerParams(vmem_limit_bytes=limit * 1024 * 1024),
        cost_estimate=pl.CostEstimate(flops=flops, bytes_accessed=bytes_accessed, transcendentals=0),
        name=name,
    )(*ins)


def shape(dims, dtype):
    return jax.ShapeDtypeStruct(dims, dtype)


def halves(x):
    high = x.astype(BF16).astype(F32)
    return high, x - high


def pack_weights(pos, lengths, labels, partner, wq, wk, wv, score, out, ids, wvs, sems):
    copies = [
        pltpu.make_async_copy(wq, out.at[0:ROWS, 0:HEAD], sems.at[0]),
        pltpu.make_async_copy(wk, out.at[0:ROWS, HEAD : 2 * HEAD], sems.at[1]),
        pltpu.make_async_copy(wv, wvs, sems.at[2]),
    ]
    for copy in copies:
        copy.start()
    z, xl, c, window = pos[0], pos[1], pos[2], pos[3]
    here = xl * 2 + c
    for n, (dz, dx) in enumerate(ORDER):
        ids[n] = ((z + dz + NZ) % NZ) * 4 + (xl ^ dx) * 2 + c
    group = z * 4 + here
    mate = partner[group]
    ids[WINDOW] = window
    ids[GROUP] = group
    for k in range(NZ):
        ids[WANTED + k] = (partner[k * 4 + here] & 3) ^ here
    ids[MATE_STEP] = mate >> 2
    for n, x in enumerate((lengths[group], lengths[mate], labels[group], labels[mate], group, mate)):
        ids[HEADS + n] = x
    ids[CORE] = c
    for n, (dy, dx) in enumerate(AROUND):
        ids[OWN + n] = (((window >> 1) + dy) & 3) * 2 + ((window & 1) ^ dx)
    for copy in copies:
        copy.wait()
    s1, rest = halves(score[...])
    s2, s3 = halves(rest)
    row = lax.broadcasted_iota(jnp.int32, (EXT, HEAD), 0)
    lhs = jnp.where(row == 0, s1, jnp.where(row == 1, s2, jnp.where(row == 2, s3, 0.0)))
    product = lax.dot_general(lhs.astype(BF16), wvs[...], LAST, preferred_element_type=F32)
    total = jnp.sum(product, axis=0, keepdims=True)
    high, low = halves(total)
    row = lax.broadcasted_iota(jnp.int32, (EXT, ROWS), 0)
    ext = jnp.where((row == 0) | (row == 2), high, jnp.where(row == 1, low, 0.0))
    out[ROWS : ROWS + EXT, :] = ext.astype(BF16)
    for h in range(2):
        start = pl.multiple_of(window * SHARE + EXT * h, EXT)
        out[ROWS + EXT : BLOCK, HEAD * h : HEAD * (h + 1)] = wvs[pl.ds(start, EXT), :]


def split_columns(hidden, out):
    size, many = 4 * BLK, 4
    i = lax.broadcasted_iota(jnp.int32, (size, size), 0)
    o = lax.broadcasted_iota(jnp.int32, (size, size), 1)
    source = BLK * ((o & 127) >> 5) + SHARE * (o >> 7) + (o & 31)
    perm = jnp.where(i == source, 1.0, 0.0).astype(BF16)
    for h in range(2):
        for first in range(0, NDP // 4, many):
            x = [
                jnp.concatenate([hidden[:, ROWS * (4 * q + k) + BLK * h :][:, :BLK] for k in range(4)], axis=1)
                for q in range(first, first + many)
            ]
            y = jnp.dot(jnp.concatenate(x, axis=0), perm, preferred_element_type=F32).astype(BF16)
            for k in range(many):
                for r in range(4):
                    out[4 * h + r, :, BLK * (first + k) : BLK * (first + k + 1)] = y[BLK * k :][:BLK, BLK * r :][:, :BLK]


def project(ids, hidden, sibling, *refs):
    count = len(ORDER)
    blocks, (out, x, w, exts, sems) = refs[:count], refs[count:]
    arrivals = []
    for n, block in enumerate(blocks):
        columns = pl.ds(pl.multiple_of(ids[n] * ROWS, ROWS), ROWS)
        at = slice(ROWS * n, ROWS * (n + 1))
        pairs = (
            (block.at[0:ROWS], w.at[at]),
            (block.at[ROWS : ROWS + EXT], exts.at[n]),
            (hidden.at[:, columns], x.at[0:BLK, at]),
            (sibling.at[:, columns], x.at[BLK : 2 * BLK, at]),
        )
        arrivals.append([pltpu.make_async_copy(a, b, sems.at[n, i]) for i, (a, b) in enumerate(pairs)])
        for copy in arrivals[n]:
            copy.start()
    acc = jnp.zeros((2 * BLK, 2 * HEAD), F32)
    wide = [jnp.zeros((BLK, BLK), F32)] * 2
    many = 4
    for first in range(0, count, many):
        for group in arrivals[first : first + many]:
            for copy in group:
                copy.wait()
        at = slice(ROWS * first, ROWS * (first + many))
        acc += jnp.dot(x[:, at], w[at, :], preferred_element_type=F32)
        for n in range(first, first + many):
            ext = exts[n].astype(F32)
            row = ext[0:1] + ext[1:2]
            for m in range(2):
                product = x[BLK * m : BLK * (m + 1), ROWS * n : ROWS * (n + 1)].astype(F32) * row
                wide[m] += product[:, 0:BLK] + product[:, BLK : 2 * BLK]
    for m in range(2):
        total = jnp.sum(wide[m].T, axis=0, keepdims=True)
        out[m, 0:BLK, :] = acc[BLK * m : BLK * (m + 1)]
        out[m, BLK : BLK + 8, :] = jnp.broadcast_to(jnp.concatenate([total, total], axis=1), (8, 2 * HEAD))


def stack_blocks(*refs):
    blocks, (out, held, sems, out_sem) = refs[: len(ORDER)], refs[len(ORDER) :]
    copies = [pltpu.make_async_copy(block, held.at[n], sems.at[n]) for n, block in enumerate(blocks)]
    for copy in copies:
        copy.start()
    for copy in copies:
        copy.wait()
    copy = pltpu.make_async_copy(held, out, out_sem.at[0])
    copy.start()
    copy.wait()


def join_cores(mine, theirs, items, first):
    row = lax.broadcasted_iota(jnp.int32, (EXT, 2 * HEAD), 0)
    for n in range(2):
        full = mine[n] + theirs[1 - n]
        high, low = halves(full[BLK : BLK + 1, 0:BLK])
        items[n, 0:BLK, :] = full[0:BLK].astype(BF16)
        items[n, BLK : BLK + EXT, :] = jnp.where(row == 0, jnp.concatenate([high, low], axis=1), 0.0).astype(BF16)
    first[...] = items[0]


def pick_for_planes(ids, near, side, out):
    for z in range(NZ):
        which = ids[WANTED + z]

        @pl.when(which < 2)
        def _(z=z, which=which):
            out[z] = near[which & 1]

        @pl.when(which >= 2)
        def _(z=z, which=which):
            out[z] = side[which & 1]


def pick_partner(ids, received, out):
    mine = received[ids[MATE_STEP]]
    for s in range(NSEQ):
        out[s] = mine


def attention(
    ids,
    mate,
    own_0,
    own_1,
    own_2,
    own_3,
    own_4,
    own_5,
    own_6,
    own_7,
    hidden,
    kept,
    swapped,
    keep,
    send,
    grads,
    crows,
    exts,
    k_t,
    q_own,
    k_own,
    q_mate,
    k_mate,
    wcol,
    scores,
    dots,
    dq,
    dk,
    cacc,
    all_grads,
    columns,
    value_parts,
    value_rows,
    shares,
    ext,
    sems,
    late_sems,
):
    pieces = [
        (mate.at[:, 0:BLK, 0:HEAD], q_mate),
        (mate.at[:, 0:BLK, HEAD : 2 * HEAD], k_mate),
        (mate.at[:, BLK : BLK + EXT, :], exts.at[0]),
    ]
    for n, ref in enumerate((own_0, own_1, own_2, own_3, own_4, own_5, own_6, own_7)):
        at = ids[OWN + n]
        pieces.append((ref.at[0:BLK, 0:HEAD], q_own.at[at]))
        pieces.append((ref.at[0:BLK, HEAD : 2 * HEAD], k_own.at[at]))
        pieces.append((ref.at[BLK : BLK + EXT, :], exts.at[1, at]))
    copies = [pltpu.make_async_copy(a, b, sems.at[n]) for n, (a, b) in enumerate(pieces)]
    for copy in copies:
        copy.start()
    late = [
        pltpu.make_async_copy(hidden, columns, late_sems.at[0]),
    ]
    for n, ref in enumerate((kept, swapped)):
        late.append(pltpu.make_async_copy(ref.at[:, ROWS + EXT : BLOCK, :], value_parts.at[n], late_sems.at[1 + n]))
    for copy in late:
        copy.start()
    cacc[...] = jnp.zeros_like(cacc)
    dk[...] = jnp.zeros_like(dk)
    for copy in copies:
        copy.wait()
    scale = 1.0 / math.sqrt(HEAD)
    exponent = scale * math.log2(math.e)
    own_len, mate_len = ids[HEADS], ids[HEADS + 1]
    for i in range(NSEQ):
        at = slice(BLK * i, BLK * (i + 1))
        k_t[:, at] = k_mate[i].astype(F32).T.astype(BF16)
        for n in range(2):
            extra = exts[n, i].astype(F32)
            row = extra[0:1, 0:BLK] + extra[0:1, BLK : 2 * BLK]
            wcol[n, at, :] = jnp.broadcast_to(row, (BLK, BLK)).T

    def softmax(side, queries, keys, start, key_len):
        q = queries[pl.ds(start // BLK, TB // BLK)].reshape(TB, HEAD)
        top = jnp.full((8, TB), -jnp.inf, F32)
        for u in range(NSEQ):
            at = slice(BLK * u, BLK * (u + 1))
            s = lax.dot_general(keys[u], q, LAST, preferred_element_type=F32)
            s = s * exponent + jnp.where(u < key_len, 0.0, -1e30).astype(F32)
            scores[side, at, :] = s
            top = jnp.maximum(top, jnp.max(s.reshape(BLK // 8, 8, TB), axis=0))
        top = jnp.max(top, axis=0, keepdims=True)
        total = jnp.zeros((8, TB), F32)
        weighed = jnp.zeros((8, TB), F32)
        for u in range(2 * NSEQ):
            at = slice(64 * u, 64 * (u + 1))
            e = jnp.exp2(scores[side, at, :] - top)
            scores[side, at, :] = e
            w = wcol[side, at, :]
            total += jnp.sum(e.reshape(8, 8, TB), axis=0)
            weighed += jnp.sum((e * jnp.concatenate([w, w], axis=1)).reshape(8, 8, TB), axis=0)
        total = jnp.sum(total, axis=0, keepdims=True)
        inverse = 1.0 / total
        s_row = jnp.sum(weighed, axis=0, keepdims=True) * inverse
        return inverse, s_row

    def live_row(start, length):
        t = lax.broadcasted_iota(jnp.int32, (1, TB), 1) + start
        return jnp.where(t < BLK * length, 1.0, 0.0).astype(F32)

    def first(n, z):
        side = 0
        start = pl.multiple_of(n * TB, TB)
        inverse, s_row = softmax(0, q_own, k_mate, start, mate_len)
        live = live_row(start, own_len)
        for u in range(2 * NSEQ):
            at = slice(64 * u, 64 * (u + 1))
            w = wcol[0, at, :]
            dots[side, at, :] = (scores[side, at, :] * (jnp.concatenate([w, w], axis=1) - s_row)).astype(BF16)
        g = jnp.dot(k_t[...], dots[side], preferred_element_type=F32)
        dq[:, pl.ds(start, TB)] = g * (inverse * live)
        return z + s_row * live

    def second(n, z):
        side = 1
        start = pl.multiple_of(n * TB, TB)
        inverse, s_row = softmax(1, q_mate, k_own, start, own_len)
        live = live_row(start, mate_len)
        r = inverse * live
        for u in range(2 * NSEQ):
            at = slice(64 * u, 64 * (u + 1))
            w = wcol[1, at, :]
            f = scores[side, at, :] * r
            cacc[at, :] += f[:, 0:BLK] + f[:, BLK:TB]
            dots[side, at, :] = (f * (jnp.concatenate([w, w], axis=1) - s_row)).astype(BF16)
        q = q_mate[pl.ds(start // BLK, TB // BLK)].reshape(TB, HEAD)
        dk[...] += jnp.dot(dots[side], q, preferred_element_type=F32)
        return z + s_row * live

    zero = jnp.zeros((1, TB), F32)

    def both(n, z):
        return first(n, z[0]), second(n, z[1])

    z_own, z_mate = lax.fori_loop(0, SEQLEN // TB, both, (zero, zero), unroll=SEQLEN // TB)

    def head(z_row, length, label, index):
        count = jnp.full((1, 1), BLK * length, jnp.int32).astype(F32)
        sign = jnp.full((1, 1), 2 * label - 1, jnp.int32).astype(F32)
        factor = 32.0 * (1.0 + 2.0 * jnp.full((1, 1), index, jnp.int32).astype(F32) / (NDP - 1))
        root = jnp.sqrt(count)
        x = -sign * (jnp.sum(z_row, axis=1, keepdims=True) / root)
        e = jnp.exp(-jnp.abs(x))
        term = factor * (jnp.maximum(x, 0.0) + jnp.log1p(e))
        sigmoid = jnp.where(x >= 0, 1.0, e) / (1.0 + e)
        return term, -factor * sign * sigmoid / root

    term, ds_own = head(z_own, own_len, ids[HEADS + 2], ids[HEADS + 4])
    _, ds_mate = head(z_mate, mate_len, ids[HEADS + 3], ids[HEADS + 5])
    row = lax.broadcasted_iota(jnp.int32, (EXT, BLK), 0)
    for i in range(NSEQ):
        at = slice(BLK * i, BLK * (i + 1))
        all_grads[0:HEAD, at] = (dq[:, at] * (ds_own * scale)).astype(BF16)
        all_grads[HEAD : 2 * HEAD, at] = (dk[at, :] * (ds_mate * scale)).T.astype(BF16)
        c_row = jnp.sum(cacc[at, :].T, axis=0, keepdims=True) * ds_mate
        high, low = halves(c_row)
        c_rows = jnp.where(row < 2, high, jnp.where(row == 2, low, 0.0)).astype(BF16)
        all_grads[2 * HEAD : 2 * HEAD + EXT, at] = c_rows

        @pl.when(ids[WINDOW] == i)
        def _(at=at, c_rows=c_rows):
            grads[...] = all_grads[0 : 2 * HEAD, at].astype(F32).T.astype(BF16)
            crows[...] = c_rows

    for copy in late:
        copy.wait()
    for flip in range(2):
        for n in range(len(ORDER)):
            for h in range(2):
                start = pl.multiple_of((ids[n] ^ flip) * SHARE + EXT * h, EXT)
                value_rows[pl.ds(start, EXT), :] = value_parts[flip, n, :, HEAD * h : HEAD * (h + 1)]
    chunk = 256
    wide = []
    for n in range(COLS // chunk):
        x = columns[:, :, chunk * n : chunk * (n + 1)].reshape(SEQLEN, chunk)
        y = jnp.dot(all_grads[...], x, preferred_element_type=F32)
        rows = y[0 : 2 * HEAD].T
        for k in range(chunk // SHARE):
            d = n * (chunk // SHARE) + k
            for h in range(2):
                part = rows[SHARE * k : SHARE * (k + 1), HEAD * h : HEAD * (h + 1)]
                shares[(d & 1) ^ ids[CORE], d >> 1, SHARE * h : SHARE * (h + 1), :] = part
        wide.append(y[2 * HEAD : 2 * HEAD + 1] + y[2 * HEAD + 2 : 2 * HEAD + 3])
    row = lax.broadcasted_iota(jnp.int32, (EXT, chunk), 0)
    gs = jnp.zeros((EXT, HEAD), F32)
    ext[...] = jnp.zeros_like(ext)
    for n, u in enumerate(wide):
        high, low = halves(u)
        ext[2 * n : 2 * n + 1, :] = u[:, 0:HEAD]
        ext[2 * n + 1 : 2 * n + 2, :] = u[:, HEAD : 2 * HEAD]
        lhs = jnp.where(row == 0, high, jnp.where(row == 1, low, 0.0)).astype(BF16)
        gs += jnp.dot(lhs, value_rows[chunk * n : chunk * (n + 1), :], preferred_element_type=F32)
    for n, total in ((8, gs[0:1] + gs[1:2]), (10, jnp.broadcast_to(term, (1, HEAD)))):
        high, low = halves(total)
        ext[n : n + 1, :] = high
        ext[n + 1 : n + 2, :] = low
    tail = ext[...]
    for m in range(NDP // 2):
        keep[m, 0 : 2 * SHARE, :] = shares[0, m]
        keep[m, 2 * SHARE : MESSAGE, :] = tail
        send[m, 0 : 2 * SHARE, :] = shares[1, m].astype(BF16)
        send[m, 2 * SHARE : MESSAGE, :] = tail.astype(BF16)


def add_core(keep, received, out, ext):
    split_again(keep[0, 2 * SHARE : MESSAGE, :] + received[0, 2 * SHARE : MESSAGE, :].astype(F32), ext)
    tail = ext[...].astype(BF16)
    for m in range(NDP // 2):
        out[m, 0 : 2 * SHARE, :] = (keep[m, 0 : 2 * SHARE, :] + received[m, 0 : 2 * SHARE, :].astype(F32)).astype(BF16)
        out[m, 2 * SHARE : MESSAGE, :] = tail


def split_again(tail, ext):
    ext[...] = tail
    for n in (8, 10):
        high, low = halves(tail[n : n + 1] + tail[n + 1 : n + 2])
        ext[n : n + 1, :] = high
        ext[n + 1 : n + 2, :] = low


def sum_shares(received, out, ext):
    acc = received[0].astype(F32)
    for n in range(1, NDP // 2):
        acc += received[n].astype(F32)
    split_again(acc[2 * SHARE : MESSAGE], ext)
    rows = acc[0 : 2 * SHARE].astype(BF16)
    tail = ext[...].astype(BF16)
    for s in range(NSEQ):
        out[s, 0 : 2 * SHARE, :] = rows
        out[s, 2 * SHARE : MESSAGE, :] = tail


def unpack(ids, received, score, gq, gk, gv, gs, loss):
    d = ids[GROUP]
    sub = lax.broadcasted_iota(jnp.int32, (8, HEAD), 0)
    lane = lax.broadcasted_iota(jnp.int32, (SHARE, HEAD), 1)
    j = lax.broadcasted_iota(jnp.int32, (SHARE, HEAD), 0)
    hit = lane == SHARE * (d & 3) + j
    readout = jnp.zeros((1, HEAD), F32)
    for s in range(NSEQ):
        at = slice(SHARE * s, SHARE * (s + 1))
        block = received[s].astype(F32)
        gq[at, :] = block[0:SHARE]
        gk[at, :] = block[SHARE : 2 * SHARE]
        tail = block[2 * SHARE : MESSAGE]
        u = jnp.sum(jnp.where(sub == d >> 2, tail[0:8], 0.0), axis=0, keepdims=True)
        column = jnp.sum(jnp.where(hit, u, 0.0), axis=1, keepdims=True)
        gv[at, :] = column * score[...]
        readout += tail[8:9] + tail[9:10]
        if s == 0:
            loss[...] = tail[10:11] + tail[11:12]
    gs[...] = readout


def hidden_grads(ids, grads, crows, kept, swapped, out):
    g = grads[...]
    c = crows[...].astype(F32).T.astype(BF16)
    for flip, ref in enumerate((kept, swapped)):
        for n in range(len(ORDER)):
            start = pl.multiple_of((ids[n] ^ flip) * ROWS, ROWS)
            y = lax.dot_general(g, ref[n, 0:ROWS, :], LAST, preferred_element_type=F32)
            y += jnp.dot(c, ref[n, ROWS : ROWS + EXT, :], preferred_element_type=F32)
            out[:, pl.ds(start, ROWS)] = y.astype(BF16)


SWAP = [(0, 1), (1, 0)]
UP = [(i, (i + 1) % NZ) for i in range(NZ)]
DOWN = [(i, (i - 1) % NZ) for i in range(NZ)]
ORDER = [(0, 0), (0, 1)]
for _step in range(1, NZ // 2 + 1):
    for _x in (0, 1):
        if _step < NZ // 2 or _x == 0:
            ORDER.append((-_step, _x))
        if _step < NZ // 2 or _x == 1:
            ORDER.append((_step, _x))


AROUND = [(0, 0), (0, 1), (1, 0), (1, 1), (-1, 0), (-1, 1), (2, 0), (2, 1)]
def ring_step(found, key):
    dz, dx = key
    step, way = (1, UP) if dz < 0 else (-1, DOWN)
    found[key] = lax.ppermute(found[(dz + step, dx)], "z", way)


def along_y(piece, dy):
    return lax.ppermute(piece, "y", [(i, (i - dy) % 4) for i in range(4)])


def per_device(hidden, w_query, w_key, w_value, score_vec, labels, lengths, partner):
    tokens = hidden.reshape(BLK, NDP * ROWS)
    score = score_vec.reshape(1, HEAD)
    z, xl, c = (lax.axis_index(a) for a in DP)
    window = lax.axis_index("y") * 2 + lax.axis_index("xh")
    pos = jnp.stack([z, xl, c, window]).astype(jnp.int32)
    item = (BLK + EXT, 2 * HEAD)

    block, ids = call(
        pack_weights,
        (shape((BLOCK, ROWS), BF16), shape((64,), jnp.int32)),
        (pos, lengths, labels, partner, w_query, w_key, w_value, score),
        far=(4, 5, 6),
        scratch=[pltpu.VMEM((ROWS, HEAD), BF16), pltpu.SemaphoreType.DMA((3,))],
        name="pack_weights",
        limit=62,
    )
    other = lax.ppermute(block, "xl", SWAP)
    sibling = lax.ppermute(tokens, "c", SWAP)
    up = lax.ppermute(block, "z", UP)
    down = lax.ppermute(block, "z", DOWN)
    later, _ = lax.optimization_barrier((tokens, block))
    split = call(split_columns, shape((NSEQ, BLK, COLS), BF16), (later,), name="split_columns", flops=1 << 30)
    split, other, up, down = lax.optimization_barrier((split, other, up, down))
    found = {(0, 0): block, (0, 1): other, (-1, 0): up, (1, 0): down}
    hidden_t = lax.all_to_all(split, SEQ, 0, 0, tiled=True)
    for key in ORDER:
        if key == (NZ // 2, 1):
            found[key] = lax.ppermute(other, "z", [(i, (i + NZ // 2) % NZ) for i in range(NZ)])
        elif key not in found:
            ring_step(found, key)
    count = len(ORDER)
    blocks = [found[key] for key in ORDER]
    partial = call(
        project,
        shape((2, BLK + 8, 2 * HEAD), F32),
        (ids, tokens, sibling, *blocks),
        far=range(1, 3 + count),
        scratch=[
            pltpu.VMEM((2 * BLK, count * ROWS), BF16),
            pltpu.VMEM((count * ROWS, ROWS), BF16),
            pltpu.VMEM((count, EXT, ROWS), BF16),
            pltpu.SemaphoreType.DMA((count, 4)),
        ],
        limit=62,
        name="project",
        flops=1 << 29,
        bytes_accessed=6 << 20,
    )
    theirs = lax.ppermute(partial, "c", SWAP)
    items, mine = call(
        join_cores, (shape((2, *item), BF16), shape(item, BF16)), (partial, theirs), name="join_cores"
    )
    side = lax.ppermute(items, "xl", SWAP)
    slots = call(
        pick_for_planes,
        shape((NZ, *item), BF16),
        (ids, items, side),
        name="pick_for_planes",
    )
    slots, hidden_t, *blocks = lax.optimization_barrier((slots, hidden_t, *blocks))
    arrived = lax.all_to_all(slots, "z", 0, 0, tiled=True)
    kept = call(
        stack_blocks,
        shape((count, BLOCK, ROWS), BF16),
        blocks,
        far=range(count),
        far_out=((count, BLOCK, ROWS),),
        scratch=[
            pltpu.VMEM((count, BLOCK, ROWS), BF16),
            pltpu.SemaphoreType.DMA((count,)),
            pltpu.SemaphoreType.DMA((1,)),
        ],
        limit=62,
        name="stack_blocks",
        bytes_accessed=5 << 20,
    )
    windows = {(0, 0): mine, (0, 1): lax.ppermute(mine, "xh", SWAP)}
    for dy in (1, -1, 2):
        for dx in (0, 1):
            windows[(dy, dx)] = along_y(windows[(0, dx)], dy)
    arrived, kept, *own = lax.optimization_barrier((arrived, kept, *[windows[key] for key in AROUND]))
    theirs = call(
        pick_partner,
        shape((NSEQ, *item), BF16),
        (ids, arrived),
        name="pick_partner",
    )
    swapped = lax.ppermute(kept, "c", SWAP)
    mate = lax.all_to_all(theirs, SEQ, 0, 0, tiled=True)

    message = (NDP // 2, MESSAGE, HEAD)
    ext = pltpu.VMEM((EXT, HEAD), F32)
    keep, send, grads, crows = call(
        attention,
        (shape(message, F32), shape(message, BF16), shape((BLK, 2 * HEAD), BF16), shape((EXT, BLK), BF16)),
        (ids, mate, *own, hidden_t, kept, swapped),
        far=range(1, 13),
        scratch=[
            pltpu.VMEM((2, NSEQ, EXT, 2 * HEAD), BF16),
            pltpu.VMEM((HEAD, SEQLEN), BF16),
            *[pltpu.VMEM((NSEQ, BLK, HEAD), BF16)] * 4,
            pltpu.VMEM((2, SEQLEN, BLK), F32),
            pltpu.VMEM((2, SEQLEN, TB), F32),
            pltpu.VMEM((2, SEQLEN, TB), BF16),
            pltpu.VMEM((HEAD, SEQLEN), F32),
            pltpu.VMEM((SEQLEN, HEAD), F32),
            pltpu.VMEM((SEQLEN, BLK), F32),
            pltpu.VMEM((2 * HEAD + EXT, SEQLEN), BF16),
            pltpu.VMEM((NSEQ, BLK, COLS), BF16),
            pltpu.VMEM((2, len(ORDER), EXT, ROWS), BF16),
            pltpu.VMEM((COLS, HEAD), BF16),
            pltpu.VMEM((2, NDP // 2, 2 * SHARE, HEAD), F32),
            ext,
            pltpu.SemaphoreType.DMA((27,)),
            pltpu.SemaphoreType.DMA((3,)),
        ],
        name="attention",
        limit=62,
        flops=1 << 31,
    )
    shares = call(add_core, shape(message, BF16), (keep, lax.ppermute(send, "c", SWAP)), scratch=[ext], name="add_core")
    arrived = lax.all_to_all(shares, ("z", "xl"), 0, 0, tiled=True)
    grad_hidden = call(
        hidden_grads,
        shape((BLK, NDP * ROWS), BF16),
        (ids, grads, crows, kept, swapped),
        name="hidden_grads",
        flops=1 << 29,
        bytes_accessed=6 << 20,
    )
    arrived, grad_hidden = lax.optimization_barrier((arrived, grad_hidden))
    sums = call(
        sum_shares,
        shape((NSEQ, MESSAGE, HEAD), BF16),
        (arrived,),
        scratch=[ext],
        name="sum_shares",
    )
    arrived = lax.all_to_all(sums, SEQ, 0, 0, tiled=True)
    grad_query, grad_key, grad_value, grad_score, loss = call(
        unpack,
        (
            shape((ROWS, HEAD), F32),
            shape((ROWS, HEAD), F32),
            shape((ROWS, HEAD), F32),
            shape((1, HEAD), F32),
            shape((1, HEAD), F32),
        ),
        (ids, arrived, score),
        name="unpack",
    )
    return (
        loss[0, 0],
        grad_query,
        grad_key,
        grad_value,
        grad_score.reshape(HEAD),
        grad_hidden.reshape(1, BLK, NDP * ROWS),
    )


def solution(mesh):
    parts = Mesh(mesh.devices.reshape(NZ, NX, NC, 4, 2), DP + SEQ)
    return jax.shard_map(
        per_device,
        mesh=parts,
        in_specs=(P(DP, SEQ, None), P(DP, None), P(DP, None), P(DP, None), P(), P(), P(), P()),
        out_specs=(P(), P(DP, None), P(DP, None), P(DP, None), P(), P(DP, SEQ, None)),
        check_vma=False,
    )
```
